768 devices in a mesh: seq: 96 (over z, x, core), head: 8 (over y).
Axes of the slice: x: 4, y: 8, z: 12, core: 2. Of those that a mesh axis runs over, the one named last changes fastest.
Arguments:
- queries: float32 [32, 12288, 128], P('head', 'seq'), may hold values from -1.75 to 1.75
- keys: float32 [32, 12288, 128], P('head', 'seq'), may hold values from -1.75 to 1.75
- values: float32 [32, 12288, 128], P('head', 'seq'), may hold values from -10 to 10
- out_grad: float32 [32, 12288, 128], P('head', 'seq'), may hold values from -6 to 6
- norm_gain: float32 [32, 128], P('head'), may hold values from 0.1 to 1.9
- log_decay: float32 [32, 12288], P('head', 'seq'), may hold values from -1.5 to 0
- doc_ids: int32 [12288], P('seq'), may hold values from 0 to 95, never falling along the last dimension, each value on 1 to 512 neighbouring positions
Outputs:
- query_grad: float32 [32, 12288, 128], P('head', 'seq')
- key_grad: float32 [32, 12288, 128], P('head', 'seq')
- value_grad: float32 [32, 12288, 128], P('head', 'seq')
The draws below stay inside these ranges and needn't reach their ends.
Inputs may be any that keep to these rules, and one draw needn't show every extreme that they name: `doc_ids`: document numbers never fall along the tokens; each document is 1 to 512 consecutive tokens, and one has exactly 512.
All inputs are finite; a program needn't handle non-finite values.
Results may differ from the reference program's by a relative error of at most 0.0003.
Values sent between devices are 32-bit elements; how exact they have to be, the bound alone decides.
No kernel may reach another device: no remote copies, remote signals or barrier semaphores. Data moves between devices by JAX's collectives and lax.ppermute only.
A program may use at most 64 MiB of HBM per device.

```python
import math
import jax
import jax.numpy as jnp
import numpy as np
from jax import lax

HEAD_DIM = 128
TOK_DEV = 128
HEADS = 32
PACKED_LENGTH = 12288
LONGEST_RECORD = 512
DOCS = 96


def draw_values(key, part):
    first_key, second_key = jax.random.split(jax.random.fold_in(key, 11))
    position = jnp.arange(HEADS, dtype=jnp.float32) / max(HEADS - 1, 1)
    entries = jax.random.truncated_normal(first_key, -4.0, 4.0, (HEADS, PACKED_LENGTH, HEAD_DIM), jnp.float32)
    rising = 0.5 * 4.0 ** position
    jitter = jax.random.uniform(second_key, (HEADS, 1, 1), jnp.float32, 0.8, 1.25)
    return entries * rising[:, None, None] * jitter


def draw_log_decay(key, part):
    base_key = jax.random.fold_in(key, 23)
    first_key, second_key, random_stream_c, fourth_key = jax.random.split(base_key, 4)
    fast_share = 0.4
    is_fast = jax.random.uniform(first_key, (HEADS, 1), jnp.float32) < fast_share
    slow_rate = 1.0 / LONGEST_RECORD
    fast_rate = 1.0 / min(40.0, TOK_DEV / 4.0)
    retention_multiplier = jnp.where(is_fast, fast_rate, slow_rate)
    attention_multiplier = jax.random.uniform(second_key, (HEADS, PACKED_LENGTH), jnp.float32, 0.5, 1.5)
    clustered_spans = jax.random.uniform(random_stream_c, (1, PACKED_LENGTH), jnp.float32) < 1.0 / LONGEST_RECORD
    objective_entries = jnp.log(jax.random.uniform(fourth_key, (1, PACKED_LENGTH), jnp.float32, 0.5, 0.8))
    return -retention_multiplier * attention_multiplier + jnp.where(clustered_spans, objective_entries, 0.0)


def level_of(key, dims, pieces, low, top_value):
    level, own = 1.0, jax.random.fold_in(key, 6)
    for dim, blocks in pieces:
        heights = jnp.exp(jax.random.uniform(jax.random.fold_in(own, dim), (blocks,), jnp.float32, low / len(pieces), top_value / len(pieces)))
        level = level * jnp.repeat(heights, dims[dim] // blocks).reshape([-1 if axis == dim else 1 for axis in range(len(dims))])
    return level


def profile(number_of, total, limit, lean):
    loads = [(1 << 20) // math.isqrt(rank ** lean) + 1 for rank in range(2, number_of + 1)]
    spare, counts = total - limit - (number_of - 1), [1] * (number_of - 1)
    while spare > 0:
        candidates = [i for i in range(number_of - 1) if counts[i] < limit]
        pool, remaining = sum([loads[i] for i in candidates]), spare
        for i in candidates:
            more = min(limit - counts[i], max(1, remaining * loads[i] // pool), spare)
            counts[i] = counts[i] + more
            spare = spare - more
    return np.array([limit] + counts)


def uneven_parts(rng, amount, total, reach, skew):
    if amount == 2:
        one = jax.random.randint(rng, (), max(1, total - reach), min(reach, total - 1) + 1)
        return jnp.stack([one, total - one])
    tallies = jnp.asarray(profile(amount, total, reach, skew), jnp.int32)
    twos = (amount - 1) // 2
    source_of, receiver = tallies[1:1 + 2 * twos:2], tallies[2:2 + 2 * twos:2]
    margin = jnp.minimum(source_of - 1, reach - receiver)
    shifted = jax.random.randint(jax.random.fold_in(rng, 1), (twos,), 0, 1 << 20) % (margin + 1)
    tallies = tallies.at[1:1 + 2 * twos:2].set(source_of - shifted).at[2:2 + 2 * twos:2].set(receiver + shifted)
    return tallies[jax.random.permutation(jax.random.fold_in(rng, 2), amount)]


def bell_draw(rng, dims, scale, bound, cuts=(), kind=jnp.bfloat16):
    values = jax.random.normal(rng, dims, jnp.float32) * scale
    if len(cuts) > 0:
        values = level_of(rng, dims, cuts, -0.22, 0.18) * values
    return jnp.clip(values, min=-bound, max=bound).astype(kind)


def setup_inputs(seed: int = 0) -> dict:
    seeds = jax.random.split(jax.random.key(seed), 8)
    return {
        "queries": bell_draw(seeds[0], (HEADS, PACKED_LENGTH, HEAD_DIM), (HEAD_DIM ** -0.25), 1.75, ((0, 8), (1, 96)), jnp.float32),
        "keys": bell_draw(seeds[1], (HEADS, PACKED_LENGTH, HEAD_DIM), (HEAD_DIM ** -0.25), 1.75, ((0, 8), (1, 96)), jnp.float32),
        "values": draw_values(jax.random.fold_in(seeds[7], 71), 0),
        "out_grad": bell_draw(seeds[3], (HEADS, PACKED_LENGTH, HEAD_DIM), 1.0, 6.0, ((0, 8), (1, 96)), jnp.float32),
        "norm_gain": jnp.clip(1.0 + 0.18 * jax.random.normal(seeds[4], (HEADS, HEAD_DIM), jnp.float32), 0.1, 1.9),
        "log_decay": draw_log_decay(jax.random.fold_in(seeds[7], 71), 0),
        "doc_ids": jnp.searchsorted(jnp.cumsum(uneven_parts(seeds[6], DOCS, PACKED_LENGTH, LONGEST_RECORD, 2)), jnp.arange(PACKED_LENGTH), side="right").astype(jnp.int32),
    }


EPSILON = 1e-06
PRECISE = lax.Precision.HIGHEST

def product(pattern, left_side, right_side):
    return jnp.einsum(pattern, left_side, right_side, precision=PRECISE, preferred_element_type=jnp.float32)

def block_weights(cumulative, labels):
    length = labels.shape[0]
    rows_iota = lax.broadcasted_iota(jnp.int32, (length, length), 0)
    cols_iota = lax.broadcasted_iota(jnp.int32, (length, length), 1)
    allowed = ((labels[:, None] == labels[None, :]) & (rows_iota >= cols_iota))[None]
    spread = cumulative[:, :, None] - cumulative[:, None, :]
    return jnp.where(allowed, jnp.exp(jnp.where(allowed, spread, 0.0)), 0.0)

def reference(queries, keys, values, out_grad, norm_gain, log_decay, doc_ids):
    queries = jnp.transpose(queries, (1, 0, 2))
    keys = jnp.transpose(keys, (1, 0, 2))
    values = jnp.transpose(values, (1, 0, 2))
    out_grad = jnp.transpose(out_grad, (1, 0, 2))
    blocks = PACKED_LENGTH // TOK_DEV
    query_blocks = queries.reshape(blocks, TOK_DEV, HEADS, HEAD_DIM)
    key_blocks = keys.reshape(blocks, TOK_DEV, HEADS, HEAD_DIM)
    value_blocks = values.reshape(blocks, TOK_DEV, HEADS, HEAD_DIM)
    decay_blocks = log_decay.reshape(HEADS, blocks, TOK_DEV).transpose(1, 0, 2)
    label_blocks = doc_ids.reshape(blocks, TOK_DEV)

    def forward_step(carried, inputs):
        prior_state, prior_label = carried
        block_queries, block_keys, block_values, block_decay, block_labels = inputs
        cumulative = jnp.cumsum(block_decay, axis=1)
        within = block_weights(cumulative, block_labels)
        scores = product('thd,shd->hts', block_queries, block_keys)
        from_prior = jnp.where((block_labels == prior_label)[:, None], jnp.exp(cumulative).T, 0.0)
        attended = product('hts,shd->thd', within * scores, block_values)
        attended = attended + from_prior[:, :, None] * product('thi,hij->thj', block_queries, prior_state)
        decay_tail = jnp.where((block_labels == block_labels[-1])[None, :], jnp.exp(cumulative[:, -1:] - cumulative), 0.0)
        kept_decay = jnp.where(block_labels[-1] == prior_label, jnp.exp(cumulative[:, -1]), 0.0)
        next_state = product('shi,shj->hij', block_keys * decay_tail.T[:, :, None], block_values)
        next_state = next_state + kept_decay[:, None, None] * prior_state
        return ((next_state, block_labels[-1]), (attended, prior_state))
    start_state = jnp.zeros((HEADS, HEAD_DIM, HEAD_DIM), jnp.float32)
    start_label = jnp.array(-1, jnp.int32)
    unused, (attended_blocks, prior_blocks) = lax.scan(forward_step, (start_state, start_label), (query_blocks, key_blocks, value_blocks, decay_blocks, label_blocks))
    attended = attended_blocks.reshape(PACKED_LENGTH, HEADS, HEAD_DIM)
    scaled_grad = norm_gain[None] * out_grad
    width_all = HEADS * HEAD_DIM
    inv_root = lax.rsqrt(lax.optimization_barrier(jnp.sum(attended * attended, axis=(1, 2))) / width_all + EPSILON)
    coupling = lax.optimization_barrier(jnp.sum(scaled_grad * attended, axis=(1, 2))) / width_all
    attn_grad = inv_root[:, None, None] * (scaled_grad - attended * (coupling * inv_root * inv_root)[:, None, None])
    grad_blocks = attn_grad.reshape(blocks, TOK_DEV, HEADS, HEAD_DIM)
    prior_labels = jnp.concatenate([jnp.array([-1], jnp.int32), label_blocks[:-1, -1]]).astype(jnp.int32)

    def grad_step(carried, inputs):
        later_state, later_label = carried
        block_queries, block_keys, block_values, block_grad, block_decay, block_labels, prior_state, prior_label = inputs
        cumulative = jnp.cumsum(block_decay, axis=1)
        within = block_weights(cumulative, block_labels)
        scores = product('thd,shd->hts', block_queries, block_keys)
        grad_weighted = within * product('thd,shd->hts', block_grad, block_values)
        from_prior = jnp.where((block_labels == prior_label)[:, None], jnp.exp(cumulative).T, 0.0)
        query_grad = product('hts,shd->thd', grad_weighted, block_keys)
        query_grad = query_grad + from_prior[:, :, None] * product('thj,hij->thi', block_grad, prior_state)
        to_next = jnp.where((block_labels == later_label)[:, None], jnp.exp(cumulative[:, -1:] - cumulative).T, 0.0)
        key_grad = product('hts,thd->shd', grad_weighted, block_queries)
        key_grad = key_grad + to_next[:, :, None] * product('hij,shj->shi', later_state, block_values)
        value_grad = product('hts,thd->shd', within * scores, block_grad)
        value_grad = value_grad + to_next[:, :, None] * product('hij,shi->shj', later_state, block_keys)
        from_start = jnp.where((block_labels == block_labels[0])[None, :], jnp.exp(cumulative), 0.0)
        kept_decay = jnp.where(block_labels[0] == later_label, jnp.exp(cumulative[:, -1]), 0.0)
        next_state = product('thi,thj->hij', block_queries * from_start.T[:, :, None], block_grad)
        next_state = next_state + kept_decay[:, None, None] * later_state
        return ((next_state, block_labels[0]), (query_grad, key_grad, value_grad))
    unused_two, (query_out, key_out, value_out) = lax.scan(grad_step, (start_state, start_label), (query_blocks, key_blocks, value_blocks, grad_blocks, decay_blocks, label_blocks, prior_blocks, prior_labels), reverse=True)
    return (jnp.transpose(query_out.reshape(PACKED_LENGTH, HEADS, HEAD_DIM), (1, 0, 2)), jnp.transpose(key_out.reshape(PACKED_LENGTH, HEADS, HEAD_DIM), (1, 0, 2)), jnp.transpose(value_out.reshape(PACKED_LENGTH, HEADS, HEAD_DIM), (1, 0, 2)))
```

```python
import functools

import jax
import jax.numpy as jnp
from jax import lax
from jax.experimental import pallas as pl
from jax.experimental.pallas import tpu as pltpu
from jax.sharding import Mesh
from jax.sharding import PartitionSpec as P

EPSILON = 1e-06
F32 = jnp.float32
BF16 = jnp.bfloat16
NN = (((1,), (0,)), ((), ()))
NT = (((1,), (1,)), ((), ()))
TN = (((0,), (0,)), ((), ()))
VMEM_LIMIT = 24 * 2**20
LAST, FIRST, EXTRA = 4, 5, 8


def split(x):
    high = x.astype(BF16)
    return high, (x - high.astype(F32)).astype(BF16)


def dot3(left, right, dims):
    one = functools.partial(lax.dot_general, dimension_numbers=dims, preferred_element_type=F32)
    return one(left[0], right[0]) + (one(left[0], right[1]) + one(left[1], right[0]))


def kernel_call(body, outs, flops):
    return pl.pallas_call(
        body,
        out_shape=outs,
        compiler_params=pltpu.CompilerParams(vmem_limit_bytes=VMEM_LIMIT),
        cost_estimate=pl.CostEstimate(flops=flops, bytes_accessed=2**20, transcendentals=0),
    )


def as_columns(row, rows):
    return jnp.broadcast_to(row, (rows, row.shape[1])).T


def lower_mask(rows):
    return lax.broadcasted_iota(jnp.int32, (rows, rows), 0) >= lax.broadcasted_iota(
        jnp.int32, (rows, rows), 1
    )


def running(lower, decay_row):
    return jnp.sum(jnp.where(lower, decay_row, 0.0), axis=1, keepdims=True)


def state_body(keys, values, decay, docs, out):
    heads, rows, width = keys.shape
    lower = lower_mask(rows)
    label_row = docs[...].astype(F32)
    label = as_columns(label_row, rows)[:, :1]
    last, first = label_row[:, rows - 1 :], label_row[:, :1]
    base = heads * rows
    for h in range(heads):
        cumulative = running(lower, decay[h : h + 1, :])
        total = cumulative[rows - 1 :, :]
        weight = jnp.where(label == last, jnp.exp(total - cumulative), 0.0)
        state = dot3(split(keys[h] * weight), split(values[h]), TN)
        out[h * width : (h + 1) * width, :] = state
        out[base + h : base + h + 1, :] = jnp.broadcast_to(total, (1, width))
    out[base + LAST : base + LAST + 1, :] = jnp.broadcast_to(last, (1, width))
    out[base + FIRST : base + FIRST + 1, :] = jnp.broadcast_to(first, (1, width))
    out[base + FIRST + 1 : base + EXTRA, :] = jnp.zeros((EXTRA - FIRST - 1, width), F32)


def chip_meta(both, out, base, heads):
    width = out.shape[1]
    out[base : base + heads, :] = both[0, base : base + heads, :] + both[1, base : base + heads, :]
    out[base + LAST : base + LAST + 1, :] = both[1, base + LAST : base + LAST + 1, :]
    out[base + FIRST : base + FIRST + 1, :] = both[0, base + FIRST : base + FIRST + 1, :]
    out[base + FIRST + 1 : base + EXTRA, :] = jnp.zeros((EXTRA - FIRST - 1, width), F32)


def row_of(ref, which, at):
    return ref[which, at : at + 1, :]


def forward_join_body(heads, both, out):
    width = out.shape[1]
    base = heads * width
    linked = row_of(both, 0, base + LAST) == row_of(both, 1, base + LAST)
    for h in range(heads):
        weight = jnp.where(linked, jnp.exp(row_of(both, 1, base + h)), 0.0)
        at = slice(h * width, (h + 1) * width)
        out[at, :] = both[1, at, :] + weight * both[0, at, :]
    chip_meta(both, out, base, heads)


def backward_join_body(heads, both, meta, out):
    width = out.shape[1]
    base = heads * width
    linked = row_of(meta, 0, base + FIRST) == row_of(meta, 1, base + FIRST)
    for h in range(heads):
        weight = jnp.where(linked, jnp.exp(row_of(meta, 0, base + h)), 0.0)
        at = slice(h * width, (h + 1) * width)
        out[at, :] = both[0, at, :] + weight * both[1, at, :]
    chip_meta(meta, out, base, heads)


def local_body(queries, keys, values, out_grad, gain, decay, docs, sent, out_local, scaled, within, weighted, started):
    del sent
    heads, rows, width = queries.shape
    lower = lower_mask(rows)
    label_row = docs[...].astype(F32)
    label = as_columns(label_row, rows)
    allowed = lower & (label == label_row)
    first = label_row[:, :1]
    for h in range(heads):
        cumulative = running(lower, decay[h : h + 1, :])
        spread = cumulative - jnp.broadcast_to(cumulative, (rows, rows)).T
        weight = jnp.where(allowed, jnp.exp(jnp.where(allowed, spread, 0.0)), 0.0)
        scores = dot3(split(queries[h]), split(keys[h]), NT)
        both = weight * scores
        within[h] = weight
        weighted[h] = both
        out_local[h] = dot3(split(both), split(values[h]), NN)
        scaled[h] = gain[h : h + 1, :] * out_grad[h]
        from_start = jnp.where(label[:, :1] == first, jnp.exp(cumulative), 0.0)
        started[h] = queries[h] * from_start


def attended_body(queries, out_local, scaled, decay, docs, core, states, arrived, attended, prior, from_prior, sums):
    heads, rows, width = queries.shape
    base = heads * width
    lower = lower_mask(rows)
    label = as_columns(docs[...].astype(F32), rows)
    second = core[0, 0] == 1
    near = row_of(arrived, 0, base + LAST)
    chained = near == row_of(arrived, 1, base + LAST)
    inner = row_of(states, 0, base + LAST)
    linked = inner == near
    ahead = jnp.where(second, inner, near)
    squares = jnp.zeros((rows, width), F32)
    inners = jnp.zeros((rows, width), F32)
    for h in range(heads):
        at = slice(h * width, (h + 1) * width)
        weight = jnp.where(chained, jnp.exp(row_of(arrived, 0, base + h)), 0.0)
        state = arrived[0, at, :] + weight * arrived[1, at, :]
        passed = jnp.where(linked, jnp.exp(row_of(states, 0, base + h)), 0.0)
        state = jnp.where(second, passed, 1.0) * state + jnp.where(second, states[0, at, :], 0.0)
        prior[h] = state
        cumulative = running(lower, decay[h : h + 1, :])
        reach = jnp.where(label == ahead, jnp.exp(cumulative), 0.0)
        from_prior[h] = reach
        value = out_local[h] + reach * dot3(split(queries[h]), split(state), NN)
        attended[h] = value
        squares += value * value
        inners += scaled[h] * value
    two = jnp.concatenate(
        [
            jnp.sum(squares.T, axis=0, keepdims=True),
            jnp.sum(inners.T, axis=0, keepdims=True),
            jnp.zeros((6, rows), F32),
        ],
        axis=0,
    )
    for i in range(sums.shape[0] // 8):
        sums[8 * i : 8 * i + 8, :] = two


def grad_state_body(width_all, sums, attended, scaled, started, grad, out):
    heads, rows, width = attended.shape
    total = sums[0:8, :]
    for i in range(1, sums.shape[0] // 8):
        total += sums[8 * i : 8 * i + 8, :]
    inverse_row = lax.rsqrt(total[0:1, :] / width_all + EPSILON)
    coupling_row = total[1:2, :] / width_all * inverse_row * inverse_row
    inverse = as_columns(inverse_row, rows)
    coupling = as_columns(coupling_row, rows)
    for h in range(heads):
        value = inverse * (scaled[h] - attended[h] * coupling)
        grad[h] = value
        out[h * width : (h + 1) * width, :] = dot3(split(started[h]), split(value), TN)


def main_grad_body(queries, keys, values, within, weighted, grad, prior, from_prior, sent, query_grad, key_local, value_local):
    del sent
    for h in range(queries.shape[0]):
        of_grad = split(grad[h])
        of_keys = split(keys[h])
        of_both = split(within[h] * dot3(of_grad, split(values[h]), NT))
        query_grad[h] = dot3(of_both, of_keys, NN) + from_prior[h] * dot3(of_grad, split(prior[h]), NT)
        key_local[h] = dot3(of_both, split(queries[h]), TN)
        value_local[h] = dot3(split(weighted[h]), of_grad, TN)


def last_grad_body(keys, values, decay, docs, core, key_local, value_local, meta, states, arrived, key_grad, value_grad):
    heads, rows, width = keys.shape
    base = heads * width
    lower = lower_mask(rows)
    label = as_columns(docs[...].astype(F32), rows)
    first = core[0, 0] == 0
    near = row_of(arrived, 0, base + FIRST)
    chained = near == row_of(arrived, 1, base + FIRST)
    inner = row_of(meta, 1, base + FIRST)
    linked = inner == near
    ahead = jnp.where(first, inner, near)
    for h in range(heads):
        at = slice(h * width, (h + 1) * width)
        weight = jnp.where(chained, jnp.exp(row_of(arrived, 0, base + h)), 0.0)
        state = arrived[0, at, :] + weight * arrived[1, at, :]
        passed = jnp.where(linked, jnp.exp(row_of(meta, 1, base + h)), 0.0)
        state = jnp.where(first, passed, 1.0) * state + jnp.where(first, states[1, at, :], 0.0)
        of_state = split(state)
        cumulative = running(lower, decay[h : h + 1, :])
        to_next = jnp.where(label == ahead, jnp.exp(cumulative[rows - 1 :, :] - cumulative), 0.0)
        key_grad[h] = key_local[h] + to_next * dot3(split(values[h]), of_state, NT)
        value_grad[h] = value_local[h] + to_next * dot3(split(keys[h]), of_state, NN)


def per_device(queries, keys, values, out_grad, norm_gain, log_decay, doc_ids):
    heads, rows, width = queries.shape
    seq = lax.axis_size("chip") * 2
    group = lax.axis_size("head")
    docs = doc_ids.reshape(1, rows)
    core = lax.axis_index("core").astype(jnp.int32).reshape(1, 1)
    shape = lambda *dims: jax.ShapeDtypeStruct(dims, F32)
    block = shape(heads, rows, width)
    payload = shape(heads * width + EXTRA, width)
    product = 6 * heads * rows * width * width

    own = kernel_call(state_body, payload, product)(keys, values, log_decay, docs)
    states = lax.all_gather(own, "core")
    chip_state = kernel_call(functools.partial(forward_join_body, heads), payload, product // 64)(states)
    ahead = [(i, i + 2 + 2 * (i % 2)) for i in range(seq)]
    moved = lax.ppermute(chip_state, ("chip", "core"), [(a, b) for a, b in ahead if b < seq])
    out_local, scaled, within, weighted, started = kernel_call(local_body, (block,) * 5, 2 * product)(
        queries, keys, values, out_grad, norm_gain, log_decay, docs, chip_state
    )
    arrived = lax.all_gather(moved, "core")
    attended, prior, from_prior, sums = kernel_call(
        attended_body, (block, block, block, shape(8 * group, rows)), product
    )(queries, out_local, scaled, log_decay, docs, core, states, arrived)
    sums = lax.all_to_all(sums, "head", 0, 0, tiled=True)
    grad, own_back = kernel_call(
        functools.partial(grad_state_body, heads * width * group), (block, shape(heads * width, width)), product
    )(sums, attended, scaled, started)
    states_back = lax.all_gather(own_back, "core")
    chip_back = kernel_call(functools.partial(backward_join_body, heads), payload, product // 64)(
        states_back, states
    )
    behind = [(i, i - 2 - 2 * (i % 2)) for i in range(seq)]
    moved_back = lax.ppermute(chip_back, ("chip", "core"), [(a, b) for a, b in behind if b >= 0])
    query_grad, key_local, value_local = kernel_call(main_grad_body, (block,) * 3, 5 * product)(
        queries, keys, values, within, weighted, grad, prior, from_prior, chip_back
    )
    arrived_back = lax.all_gather(moved_back, "core")
    key_grad, value_grad = kernel_call(last_grad_body, (block,) * 2, 2 * product)(
        keys, values, log_decay, docs, core, key_local, value_local, states, states_back, arrived_back
    )
    return query_grad, key_grad, value_grad


def solution(mesh):
    seq, head = mesh.devices.shape
    fine = Mesh(mesh.devices.reshape(seq // 2, 2, head), ("chip", "core", "head"))
    tokens = ("chip", "core")
    block = P("head", tokens, None)
    return jax.shard_map(
        per_device,
        mesh=fine,
        in_specs=(block, block, block, block, P("head", None), P("head", tokens), P(tokens)),
        out_specs=(block, block, block),
        check_vma=False,
    )
```

```python
import functools

import jax
import jax.numpy as jnp
from jax import lax
from jax.experimental import pallas as pl
from jax.experimental.pallas import tpu as pltpu
from jax.sharding import Mesh
from jax.sharding import PartitionSpec as P

EPSILON = 1e-06
F32 = jnp.float32
BF16 = jnp.bfloat16
NN = (((1,), (0,)), ((), ()))
NT = (((1,), (1,)), ((), ()))
TN = (((0,), (0,)), ((), ()))
VMEM_LIMIT = 24 * 2**20
LAST, FIRST, EXTRA = 4, 5, 8


def split(x):
    high = x.astype(BF16)
    return high, (x - high.astype(F32)).astype(BF16)


def dot3(left, right, dims):
    one = functools.partial(lax.dot_general, dimension_numbers=dims, preferred_element_type=F32)
    return one(left[0], right[0]) + (one(left[0], right[1]) + one(left[1], right[0]))


def kernel_call(body, outs, flops, kinds="", out_kinds="", scratch=()):
    spaces = {"h": pltpu.HBM, "s": pltpu.SMEM, "v": pltpu.VMEM}

    def call(*operands):
        of = [pl.BlockSpec(memory_space=spaces[c]) for c in kinds.ljust(len(operands), "v")]
        more = {}
        if out_kinds:
            made = [pl.BlockSpec(memory_space=spaces[c]) for c in out_kinds]
            more["out_specs"] = tuple(made)
        return pl.pallas_call(
            body,
            out_shape=outs,
            in_specs=of,
            scratch_shapes=list(scratch),
            compiler_params=pltpu.CompilerParams(vmem_limit_bytes=VMEM_LIMIT),
            cost_estimate=pl.CostEstimate(flops=flops, bytes_accessed=2**20, transcendentals=0),
            **more,
        )(*operands)

    return call


def as_columns(row, rows):
    return jnp.broadcast_to(row, (rows, row.shape[1])).T


def lower_mask(rows):
    return lax.broadcasted_iota(jnp.int32, (rows, rows), 0) >= lax.broadcasted_iota(
        jnp.int32, (rows, rows), 1
    )


def running(lower, decay_row):
    return jnp.sum(jnp.where(lower, decay_row, 0.0), axis=1, keepdims=True)


def state_body(
    queries_hbm, keys_hbm, values_hbm, cotangent_hbm, gain_hbm, decay_hbm, docs_hbm,
    out, queries, keys, values, cotangent, gain, decay, docs, arrival,
):
    heads, rows, width = keys.shape
    pairs = [(docs_hbm, docs), (decay_hbm, decay)]
    for h in range(heads):
        pairs += [(keys_hbm.at[h], keys.at[h]), (values_hbm.at[h], values.at[h])]
    pairs += [(gain_hbm, gain), (queries_hbm, queries), (cotangent_hbm, cotangent)]
    copies = [pltpu.make_async_copy(a, b, arrival.at[i]) for i, (a, b) in enumerate(pairs)]
    for copy in copies:
        copy.start()
    lower = lower_mask(rows)
    base = heads * rows
    copies[0].wait()
    label_row = docs[...].astype(F32)
    label = as_columns(label_row, rows)[:, :1]
    last, first = label_row[:, rows - 1 :], label_row[:, :1]
    out[base + LAST : base + LAST + 1, :] = jnp.broadcast_to(last, (1, width))
    out[base + FIRST : base + FIRST + 1, :] = jnp.broadcast_to(first, (1, width))
    out[base + FIRST + 1 : base + EXTRA, :] = jnp.zeros((EXTRA - FIRST - 1, width), F32)
    copies[1].wait()
    weights = []
    for h in range(heads):
        cumulative = running(lower, decay[h : h + 1, :])
        total = cumulative[rows - 1 :, :]
        weights.append(jnp.where(label == last, jnp.exp(total - cumulative), 0.0))
        out[base + h : base + h + 1, :] = jnp.broadcast_to(total, (1, width))
    for h in range(heads):
        copies[2 + 2 * h].wait()
        copies[3 + 2 * h].wait()
        state = dot3(split(keys[h] * weights[h]), split(values[h]), TN)
        out[h * width : (h + 1) * width, :] = state
    for copy in copies[2 + 2 * heads :]:
        copy.wait()


def chip_meta(both, out, base, heads):
    width = out.shape[1]
    out[base : base + heads, :] = both[0, base : base + heads, :] + both[1, base : base + heads, :]
    out[base + LAST : base + LAST + 1, :] = both[1, base + LAST : base + LAST + 1, :]
    out[base + FIRST : base + FIRST + 1, :] = both[0, base + FIRST : base + FIRST + 1, :]
    out[base + FIRST + 1 : base + EXTRA, :] = jnp.zeros((EXTRA - FIRST - 1, width), F32)


def row_of(ref, which, at):
    return ref[which, at : at + 1, :]


def forward_join_body(heads, both, out):
    width = out.shape[1]
    base = heads * width
    linked = row_of(both, 0, base + LAST) == row_of(both, 1, base + LAST)
    for h in range(heads):
        weight = jnp.where(linked, jnp.exp(row_of(both, 1, base + h)), 0.0)
        at = slice(h * width, (h + 1) * width)
        out[at, :] = both[1, at, :] + weight * both[0, at, :]
    chip_meta(both, out, base, heads)


def backward_join_body(heads, both, meta, out):
    width = out.shape[1]
    base = heads * width
    linked = row_of(meta, 0, base + FIRST) == row_of(meta, 1, base + FIRST)
    for h in range(heads):
        weight = jnp.where(linked, jnp.exp(row_of(meta, 0, base + h)), 0.0)
        at = slice(h * width, (h + 1) * width)
        out[at, :] = both[0, at, :] + weight * both[1, at, :]
    chip_meta(meta, out, base, heads)


def local_body(queries, keys, values, out_grad, gain, decay, docs, sent, out_local, scaled, within, weighted, started):
    del sent
    heads, rows, width = queries.shape
    lower = lower_mask(rows)
    label_row = docs[...].astype(F32)
    label = as_columns(label_row, rows)
    allowed = lower & (label == label_row)
    first = label_row[:, :1]
    for h in range(heads):
        cumulative = running(lower, decay[h : h + 1, :])
        spread = cumulative - jnp.broadcast_to(cumulative, (rows, rows)).T
        weight = jnp.where(allowed, jnp.exp(jnp.where(allowed, spread, 0.0)), 0.0)
        scores = dot3(split(queries[h]), split(keys[h]), NT)
        both = weight * scores
        within[h] = weight
        weighted[h] = both
        out_local[h] = dot3(split(both), split(values[h]), NN)
        scaled[h] = gain[h : h + 1, :] * out_grad[h]
        from_start = jnp.where(label[:, :1] == first, jnp.exp(cumulative), 0.0)
        started[h] = queries[h] * from_start


def attended_body(core, queries, out_local, scaled, decay, docs, states, arrived, attended, prior, from_prior, sums):
    heads, rows, width = queries.shape
    base = heads * width
    lower = lower_mask(rows)
    label = as_columns(docs[...].astype(F32), rows)
    second = core[0, 0] == 1
    near = row_of(arrived, 0, base + LAST)
    chained = near == row_of(arrived, 1, base + LAST)
    inner = row_of(states, 0, base + LAST)
    linked = inner == near
    ahead = jnp.where(second, inner, near)
    squares = jnp.zeros((rows, width), F32)
    inners = jnp.zeros((rows, width), F32)
    for h in range(heads):
        at = slice(h * width, (h + 1) * width)
        weight = jnp.where(chained, jnp.exp(row_of(arrived, 0, base + h)), 0.0)
        state = arrived[0, at, :] + weight * arrived[1, at, :]
        passed = jnp.where(linked, jnp.exp(row_of(states, 0, base + h)), 0.0)
        state = jnp.where(second, passed, 1.0) * state + jnp.where(second, states[0, at, :], 0.0)
        prior[h] = state
        cumulative = running(lower, decay[h : h + 1, :])
        reach = jnp.where(label == ahead, jnp.exp(cumulative), 0.0)
        from_prior[h] = reach
        value = out_local[h] + reach * dot3(split(queries[h]), split(state), NN)
        attended[h] = value
        squares += value * value
        inners += scaled[h] * value
    two = jnp.concatenate(
        [
            jnp.sum(squares.T, axis=0, keepdims=True),
            jnp.sum(inners.T, axis=0, keepdims=True),
            jnp.zeros((6, rows), F32),
        ],
        axis=0,
    )
    for i in range(sums.shape[0] // 8):
        sums[8 * i : 8 * i + 8, :] = two


def grad_state_body(width_all, sums, attended, scaled, started, grad, out):
    heads, rows, width = attended.shape
    total = sums[0:8, :]
    for i in range(1, sums.shape[0] // 8):
        total += sums[8 * i : 8 * i + 8, :]
    inverse_row = lax.rsqrt(total[0:1, :] / width_all + EPSILON)
    coupling_row = total[1:2, :] / width_all * inverse_row * inverse_row
    inverse = as_columns(inverse_row, rows)
    coupling = as_columns(coupling_row, rows)
    for h in range(heads):
        value = inverse * (scaled[h] - attended[h] * coupling)
        grad[h] = value
        out[h * width : (h + 1) * width, :] = dot3(split(started[h]), split(value), TN)


def main_grad_body(queries, keys, values, within, weighted, grad, prior, from_prior, sent, query_grad, key_local, value_local):
    del sent
    for h in range(queries.shape[0]):
        of_grad = split(grad[h])
        of_keys = split(keys[h])
        of_both = split(within[h] * dot3(of_grad, split(values[h]), NT))
        query_grad[h] = dot3(of_both, of_keys, NN) + from_prior[h] * dot3(of_grad, split(prior[h]), NT)
        key_local[h] = dot3(of_both, split(queries[h]), TN)
        value_local[h] = dot3(split(weighted[h]), of_grad, TN)


def last_grad_body(
    core, keys, values, decay, docs, key_local, value_local, meta, states, arrived,
    key_grad_hbm, value_grad_hbm, key_grad, value_grad, sent,
):
    heads, rows, width = keys.shape
    base = heads * width
    lower = lower_mask(rows)
    first = core[0, 0] == 0
    near = row_of(arrived, 0, base + FIRST)
    chained = near == row_of(arrived, 1, base + FIRST)
    inner = row_of(meta, 1, base + FIRST)
    linked = inner == near
    ahead = as_columns(docs[...].astype(F32), rows) == jnp.where(first, inner, near)
    copies = []
    for h in range(heads):
        at = slice(h * width, (h + 1) * width)
        weight = jnp.where(chained, jnp.exp(row_of(arrived, 0, base + h)), 0.0)
        state = arrived[0, at, :] + weight * arrived[1, at, :]
        passed = jnp.where(linked, jnp.exp(row_of(meta, 1, base + h)), 0.0)
        of_state = split(jnp.where(first, states[1, at, :] + passed * state, state))
        cumulative = running(lower, decay[h : h + 1, :])
        to_next = jnp.where(ahead, jnp.exp(cumulative[rows - 1 :, :] - cumulative), 0.0)
        key_grad[h] = key_local[h] + to_next * dot3(split(values[h]), of_state, NT)
        value_grad[h] = value_local[h] + to_next * dot3(split(keys[h]), of_state, NN)
        for i, (a, b) in enumerate(((key_grad, key_grad_hbm), (value_grad, value_grad_hbm))):
            copies.append(pltpu.make_async_copy(a.at[h], b.at[h], sent.at[2 * h + i]))
            copies[-1].start()
    for copy in copies:
        copy.wait()


def per_device(queries, keys, values, out_grad, norm_gain, log_decay, doc_ids):
    heads, rows, width = queries.shape
    seq = lax.axis_size("chip") * 2
    group = lax.axis_size("head")
    docs = doc_ids.reshape(1, rows)
    core = lax.axis_index("core").astype(jnp.int32).reshape(1, 1)
    shape = lambda *dims: jax.ShapeDtypeStruct(dims, F32)
    block = shape(heads, rows, width)
    payload = shape(heads * width + EXTRA, width)
    product = 6 * heads * rows * width * width

    given = [queries, keys, values, out_grad, norm_gain, log_decay, docs]
    own, queries, keys, values, out_grad, norm_gain, log_decay, docs = kernel_call(
        state_body,
        (payload, *(jax.ShapeDtypeStruct(a.shape, a.dtype) for a in given)),
        product,
        "h" * len(given),
        scratch=(pltpu.SemaphoreType.DMA((2 * heads + 5,)),),
    )(*(pltpu.with_memory_space_constraint(a, pltpu.HBM) for a in given))
    states = lax.all_gather(own, "core")
    chip_state = kernel_call(functools.partial(forward_join_body, heads), payload, product // 64)(states)
    ahead = [(i, i + 2 + 2 * (i % 2)) for i in range(seq)]
    moved = lax.ppermute(chip_state, ("chip", "core"), [(a, b) for a, b in ahead if b < seq])
    out_local, scaled, within, weighted, started = kernel_call(local_body, (block,) * 5, 2 * product)(
        queries, keys, values, out_grad, norm_gain, log_decay, docs, chip_state
    )
    arrived = lax.all_gather(moved, "core")
    attended, prior, from_prior, sums = kernel_call(
        attended_body, (block, block, block, shape(8 * group, rows)), product, "s"
    )(core, queries, out_local, scaled, log_decay, docs, states, arrived)
    sums = lax.all_to_all(sums, "head", 0, 0, tiled=True)
    grad, own_back = kernel_call(
        functools.partial(grad_state_body, heads * width * group), (block, shape(heads * width, width)), product
    )(sums, attended, scaled, started)
    states_back = lax.all_gather(own_back, "core")
    chip_back = kernel_call(functools.partial(backward_join_body, heads), payload, product // 64)(
        states_back, states
    )
    behind = [(i, i - 2 - 2 * (i % 2)) for i in range(seq)]
    moved_back = lax.ppermute(chip_back, ("chip", "core"), [(a, b) for a, b in behind if b >= 0])
    query_grad, key_local, value_local = kernel_call(main_grad_body, (block,) * 3, 5 * product)(
        queries, keys, values, within, weighted, grad, prior, from_prior, chip_back
    )
    arrived_back = lax.all_gather(moved_back, "core")
    held = pltpu.VMEM((heads, rows, width), F32)
    key_grad, value_grad = kernel_call(
        last_grad_body,
        (block,) * 2,
        2 * product,
        "s",
        "hh",
        (held, held, pltpu.SemaphoreType.DMA((2 * heads,))),
    )(core, keys, values, log_decay, docs, key_local, value_local, states, states_back, arrived_back)
    return query_grad, key_grad, value_grad


def solution(mesh):
    seq, head = mesh.devices.shape
    fine = Mesh(mesh.devices.reshape(seq // 2, 2, head), ("chip", "core", "head"))
    tokens = ("chip", "core")
    block = P("head", tokens, None)
    return jax.shard_map(
        per_device,
        mesh=fine,
        in_specs=(block, block, block, block, P("head", None), P("head", tokens), P(tokens)),
        out_specs=(block, block, block),
        check_vma=False,
    )
```

```python
import functools

import jax
import jax.numpy as jnp
from jax import lax
from jax.experimental import pallas as pl
from jax.experimental.pallas import tpu as pltpu
from jax.sharding import Mesh
from jax.sharding import PartitionSpec as P

EPSILON = 1e-06
F32 = jnp.float32
BF16 = jnp.bfloat16
NN = (((1,), (0,)), ((), ()))
NT = (((1,), (1,)), ((), ()))
TN = (((0,), (0,)), ((), ()))
VMEM_LIMIT = 24 * 2**20
LAST, FIRST, EXTRA = 4, 5, 8


def split(x):
    high = x.astype(BF16)
    return high, (x - high.astype(F32)).astype(BF16)


def dot3(left, right, dims):
    one = functools.partial(lax.dot_general, dimension_numbers=dims, preferred_element_type=F32)
    return one(left[0], right[0]) + (one(left[0], right[1]) + one(left[1], right[0]))


def kernel_call(body, outs, flops, kinds="", out_kinds="", scratch=()):
    spaces = {"h": pltpu.HBM, "s": pltpu.SMEM, "v": pltpu.VMEM}

    def call(*operands):
        of = [pl.BlockSpec(memory_space=spaces[c]) for c in kinds.ljust(len(operands), "v")]
        more = {}
        if out_kinds:
            made = [pl.BlockSpec(memory_space=spaces[c]) for c in out_kinds]
            more["out_specs"] = tuple(made)
        return pl.pallas_call(
            body,
            out_shape=outs,
            in_specs=of,
            scratch_shapes=list(scratch),
            compiler_params=pltpu.CompilerParams(vmem_limit_bytes=VMEM_LIMIT),
            cost_estimate=pl.CostEstimate(flops=flops, bytes_accessed=2**20, transcendentals=0),
            **more,
        )(*operands)

    return call


def as_columns(row, rows):
    return jnp.broadcast_to(row, (rows, row.shape[1])).T


def lower_mask(rows):
    return lax.broadcasted_iota(jnp.int32, (rows, rows), 0) >= lax.broadcasted_iota(
        jnp.int32, (rows, rows), 1
    )


def running(lower, decay_row):
    return jnp.sum(jnp.where(lower, decay_row, 0.0), axis=1, keepdims=True)


def state_body(
    keys_hbm, values_hbm, gain_hbm, decay_hbm, docs_hbm,
    out, keys, values, gain, decay, docs, arrival,
):
    heads, rows, width = keys.shape
    pairs = [(docs_hbm, docs), (decay_hbm, decay)]
    for h in range(heads):
        pairs += [(keys_hbm.at[h], keys.at[h]), (values_hbm.at[h], values.at[h])]
    pairs.append((gain_hbm, gain))
    copies = [pltpu.make_async_copy(a, b, arrival.at[i]) for i, (a, b) in enumerate(pairs)]
    for copy in copies:
        copy.start()
    lower = lower_mask(rows)
    base = heads * rows
    copies[0].wait()
    label_row = docs[...].astype(F32)
    label = as_columns(label_row, rows)[:, :1]
    last, first = label_row[:, rows - 1 :], label_row[:, :1]
    out[base + LAST : base + LAST + 1, :] = jnp.broadcast_to(last, (1, width))
    out[base + FIRST : base + FIRST + 1, :] = jnp.broadcast_to(first, (1, width))
    out[base + FIRST + 1 : base + EXTRA, :] = jnp.zeros((EXTRA - FIRST - 1, width), F32)
    copies[1].wait()
    weights = []
    for h in range(heads):
        cumulative = running(lower, decay[h : h + 1, :])
        total = cumulative[rows - 1 :, :]
        weights.append(jnp.where(label == last, jnp.exp(total - cumulative), 0.0))
        out[base + h : base + h + 1, :] = jnp.broadcast_to(total, (1, width))
    for h in range(heads):
        copies[2 + 2 * h].wait()
        copies[3 + 2 * h].wait()
        state = dot3(split(keys[h] * weights[h]), split(values[h]), TN)
        out[h * width : (h + 1) * width, :] = state
    for copy in copies[2 + 2 * heads :]:
        copy.wait()


def chip_meta(both, out, base, heads):
    width = out.shape[1]
    out[base : base + heads, :] = both[0, base : base + heads, :] + both[1, base : base + heads, :]
    out[base + LAST : base + LAST + 1, :] = both[1, base + LAST : base + LAST + 1, :]
    out[base + FIRST : base + FIRST + 1, :] = both[0, base + FIRST : base + FIRST + 1, :]
    out[base + FIRST + 1 : base + EXTRA, :] = jnp.zeros((EXTRA - FIRST - 1, width), F32)


def row_of(ref, which, at):
    return ref[which, at : at + 1, :]


def forward_join_body(heads, both, out):
    width = out.shape[1]
    base = heads * width
    linked = row_of(both, 0, base + LAST) == row_of(both, 1, base + LAST)
    for h in range(heads):
        weight = jnp.where(linked, jnp.exp(row_of(both, 1, base + h)), 0.0)
        at = slice(h * width, (h + 1) * width)
        out[at, :] = both[1, at, :] + weight * both[0, at, :]
    chip_meta(both, out, base, heads)


def backward_join_body(heads, both, meta, out):
    width = out.shape[1]
    base = heads * width
    linked = row_of(meta, 0, base + FIRST) == row_of(meta, 1, base + FIRST)
    for h in range(heads):
        weight = jnp.where(linked, jnp.exp(row_of(meta, 0, base + h)), 0.0)
        at = slice(h * width, (h + 1) * width)
        out[at, :] = both[0, at, :] + weight * both[1, at, :]
    chip_meta(meta, out, base, heads)


def local_body(queries, keys, values, out_grad, gain, decay, docs, sent, out_local, scaled, within, weighted, started):
    del sent
    heads, rows, width = queries.shape
    lower = lower_mask(rows)
    label_row = docs[...].astype(F32)
    label = as_columns(label_row, rows)
    allowed = lower & (label == label_row)
    first = label_row[:, :1]
    for h in range(heads):
        cumulative = running(lower, decay[h : h + 1, :])
        spread = cumulative - jnp.broadcast_to(cumulative, (rows, rows)).T
        weight = jnp.where(allowed, jnp.exp(jnp.where(allowed, spread, 0.0)), 0.0)
        scores = dot3(split(queries[h]), split(keys[h]), NT)
        both = weight * scores
        within[h] = weight
        weighted[h] = both
        out_local[h] = dot3(split(both), split(values[h]), NN)
        scaled[h] = gain[h : h + 1, :] * out_grad[h]
        from_start = jnp.where(label[:, :1] == first, jnp.exp(cumulative), 0.0)
        started[h] = queries[h] * from_start


def attended_body(core, queries, out_local, scaled, decay, docs, states, arrived, attended, prior, from_prior, sums):
    heads, rows, width = queries.shape
    base = heads * width
    lower = lower_mask(rows)
    label = as_columns(docs[...].astype(F32), rows)
    second = core[0, 0] == 1
    near = row_of(arrived, 0, base + LAST)
    chained = near == row_of(arrived, 1, base + LAST)
    inner = row_of(states, 0, base + LAST)
    linked = inner == near
    ahead = jnp.where(second, inner, near)
    squares = jnp.zeros((rows, width), F32)
    inners = jnp.zeros((rows, width), F32)
    for h in range(heads):
        at = slice(h * width, (h + 1) * width)
        weight = jnp.where(chained, jnp.exp(row_of(arrived, 0, base + h)), 0.0)
        state = arrived[0, at, :] + weight * arrived[1, at, :]
        passed = jnp.where(linked, jnp.exp(row_of(states, 0, base + h)), 0.0)
        state = jnp.where(second, passed, 1.0) * state + jnp.where(second, states[0, at, :], 0.0)
        prior[h] = state
        cumulative = running(lower, decay[h : h + 1, :])
        reach = jnp.where(label == ahead, jnp.exp(cumulative), 0.0)
        from_prior[h] = reach
        value = out_local[h] + reach * dot3(split(queries[h]), split(state), NN)
        attended[h] = value
        squares += value * value
        inners += scaled[h] * value
    two = jnp.concatenate(
        [
            jnp.sum(squares.T, axis=0, keepdims=True),
            jnp.sum(inners.T, axis=0, keepdims=True),
        ],
        axis=0,
    )
    for i in range(sums.shape[0]):
        sums[i] = two


def grad_state_body(width_all, sums, attended, scaled, started, grad, out):
    heads, rows, width = attended.shape
    total = jnp.sum(sums[...], axis=0)
    inverse_row = lax.rsqrt(total[0:1, :] / width_all + EPSILON)
    coupling_row = total[1:2, :] / width_all * inverse_row * inverse_row
    inverse = as_columns(inverse_row, rows)
    coupling = as_columns(coupling_row, rows)
    for h in range(heads):
        value = inverse * (scaled[h] - attended[h] * coupling)
        grad[h] = value
        out[h * width : (h + 1) * width, :] = dot3(split(started[h]), split(value), TN)


def main_grad_body(
    queries, keys, values, decay, within, weighted, grad, prior, from_prior, sent,
    query_grad, key_local, value_local, tails, *halves,
):
    del sent
    lower = lower_mask(queries.shape[1])
    for h in range(queries.shape[0]):
        of_grad = split(grad[h])
        of_keys = split(keys[h])
        of_values = split(values[h])
        of_both = split(within[h] * dot3(of_grad, of_values, NT))
        query_grad[h] = dot3(of_both, of_keys, NN) + from_prior[h] * dot3(of_grad, split(prior[h]), NT)
        key_local[h] = dot3(of_both, split(queries[h]), TN)
        value_local[h] = dot3(split(weighted[h]), of_grad, TN)
        for half, part in zip(halves, (*of_keys, *of_values)):
            half[h] = part
        cumulative = running(lower, decay[h : h + 1, :])
        tail = jnp.exp(cumulative[queries.shape[1] - 1 :, :] - cumulative)
        tails[h] = jnp.broadcast_to(tail, tails.shape[1:])


def last_grad_body(
    core, keys_high, keys_low, values_high, values_low, tails, docs, key_local, value_local,
    meta, states, arrived, key_grad_hbm, value_grad_hbm, key_grad, value_grad, sent,
):
    heads, rows, width = tails.shape
    base = heads * width
    first = core[0, 0] == 0
    near = row_of(arrived, 0, base + FIRST)
    chained = near == row_of(arrived, 1, base + FIRST)
    inner = row_of(meta, 1, base + FIRST)
    linked = inner == near
    ahead = as_columns(docs[...].astype(F32), rows) == jnp.where(first, inner, near)
    copies = []
    for h in range(heads):
        at = slice(h * width, (h + 1) * width)
        weight = jnp.where(chained, jnp.exp(row_of(arrived, 0, base + h)), 0.0)
        state = arrived[0, at, :] + weight * arrived[1, at, :]
        passed = jnp.where(linked, jnp.exp(row_of(meta, 1, base + h)), 0.0)
        of_state = split(jnp.where(first, states[1, at, :] + passed * state, state))
        to_next = jnp.where(ahead, tails[h], 0.0)
        key_grad[h] = key_local[h] + to_next * dot3((values_high[h], values_low[h]), of_state, NT)
        value_grad[h] = value_local[h] + to_next * dot3((keys_high[h], keys_low[h]), of_state, NN)
        for i, (a, b) in enumerate(((key_grad, key_grad_hbm), (value_grad, value_grad_hbm))):
            copies.append(pltpu.make_async_copy(a.at[h], b.at[h], sent.at[2 * h + i]))
            copies[-1].start()
    for copy in copies:
        copy.wait()


def per_device(queries, keys, values, out_grad, norm_gain, log_decay, doc_ids):
    heads, rows, width = queries.shape
    seq = lax.axis_size("chip") * 2
    group = lax.axis_size("head")
    docs = doc_ids.reshape(1, rows)
    core = lax.axis_index("core").astype(jnp.int32).reshape(1, 1)
    shape = lambda *dims: jax.ShapeDtypeStruct(dims, F32)
    block = shape(heads, rows, width)
    payload = shape(heads * width + EXTRA, width)
    product = 6 * heads * rows * width * width

    given = [keys, values, norm_gain, log_decay, docs]
    own, keys, values, norm_gain, log_decay, docs = kernel_call(
        state_body,
        (payload, *(jax.ShapeDtypeStruct(a.shape, a.dtype) for a in given)),
        product,
        "h" * len(given),
        scratch=(pltpu.SemaphoreType.DMA((2 * heads + 3,)),),
    )(*(pltpu.with_memory_space_constraint(a, pltpu.HBM) for a in given))
    states = lax.all_gather(own, "core")
    chip_state = kernel_call(functools.partial(forward_join_body, heads), payload, product // 64)(states)
    ahead = [(i, i + 2 + 2 * (i % 2)) for i in range(seq)]
    moved = lax.ppermute(chip_state, ("chip", "core"), [(a, b) for a, b in ahead if b < seq])
    out_local, scaled, within, weighted, started = kernel_call(local_body, (block,) * 5, 2 * product)(
        queries, keys, values, out_grad, norm_gain, log_decay, docs, chip_state
    )
    arrived = lax.all_gather(moved, "core")
    attended, prior, from_prior, sums = kernel_call(
        attended_body, (block, block, block, shape(group, 2, rows)), product, "s"
    )(core, queries, out_local, scaled, log_decay, docs, states, arrived)
    sums = lax.all_to_all(sums, "head", 0, 0, tiled=True)
    grad, own_back = kernel_call(
        functools.partial(grad_state_body, heads * width * group), (block, shape(heads * width, width)), product
    )(sums, attended, scaled, started)
    states_back = lax.all_gather(own_back, "core")
    chip_back = kernel_call(functools.partial(backward_join_body, heads), payload, product // 64)(
        states_back, states
    )
    behind = [(i, i - 2 - 2 * (i % 2)) for i in range(seq)]
    moved_back = lax.ppermute(chip_back, ("chip", "core"), [(a, b) for a, b in behind if b >= 0])
    half = jax.ShapeDtypeStruct((heads, rows, width), BF16)
    query_grad, key_local, value_local, tails, *halves = kernel_call(
        main_grad_body, (block,) * 4 + (half,) * 4, 5 * product
    )(
        queries, keys, values, log_decay, within, weighted, grad, prior, from_prior, chip_back
    )
    arrived_back = lax.all_gather(moved_back, "core")
    held = pltpu.VMEM((heads, rows, width), F32)
    key_grad, value_grad = kernel_call(
        last_grad_body,
        (block,) * 2,
        2 * product,
        "s",
        "hh",
        (held, held, pltpu.SemaphoreType.DMA((2 * heads,))),
    )(core, *halves, tails, docs, key_local, value_local, states, states_back, arrived_back)
    return query_grad, key_grad, value_grad


def solution(mesh):
    seq, head = mesh.devices.shape
    fine = Mesh(mesh.devices.reshape(seq // 2, 2, head), ("chip", "core", "head"))
    tokens = ("chip", "core")
    block = P("head", tokens, None)
    return jax.shard_map(
        per_device,
        mesh=fine,
        in_specs=(block, block, block, block, P("head", None), P("head", tokens), P(tokens)),
        out_specs=(block, block, block),
        check_vma=False,
    )
```

```python
import functools

import jax
import jax.numpy as jnp
from jax import lax
from jax.experimental import pallas as pl
from jax.experimental.pallas import tpu as pltpu
from jax.sharding import Mesh
from jax.sharding import PartitionSpec as P

EPSILON = 1e-06
F32 = jnp.float32
BF16 = jnp.bfloat16
NN = (((1,), (0,)), ((), ()))
NT = (((1,), (1,)), ((), ()))
TN = (((0,), (0,)), ((), ()))
VMEM_LIMIT = 12 * 2**20
LAST, FIRST, EXTRA = 4, 5, 8


def split(x):
    high = x.astype(BF16)
    return high, (x - high.astype(F32)).astype(BF16)


def dot3(left, right, dims):
    one = functools.partial(lax.dot_general, dimension_numbers=dims, preferred_element_type=F32)
    return one(left[0], right[0]) + (one(left[0], right[1]) + one(left[1], right[0]))


def kernel_call(body, outs, flops, kinds="", out_kinds="", scratch=()):
    spaces = {"h": pltpu.HBM, "s": pltpu.SMEM, "v": pltpu.VMEM}

    def call(*operands):
        of = [pl.BlockSpec(memory_space=spaces[c]) for c in kinds.ljust(len(operands), "v")]
        more = {}
        if out_kinds:
            made = [pl.BlockSpec(memory_space=spaces[c]) for c in out_kinds]
            more["out_specs"] = tuple(made)
        return pl.pallas_call(
            body,
            out_shape=outs,
            in_specs=of,
            scratch_shapes=list(scratch),
            compiler_params=pltpu.CompilerParams(vmem_limit_bytes=VMEM_LIMIT),
            cost_estimate=pl.CostEstimate(flops=flops, bytes_accessed=2**20, transcendentals=0),
            **more,
        )(*operands)

    return call


def as_columns(row, rows):
    return jnp.broadcast_to(row, (rows, row.shape[1])).T


def lower_mask(rows):
    return lax.broadcasted_iota(jnp.int32, (rows, rows), 0) >= lax.broadcasted_iota(
        jnp.int32, (rows, rows), 1
    )


def running(lower, decay_row):
    return jnp.sum(jnp.where(lower, decay_row, 0.0), axis=1, keepdims=True)


def state_body(
    keys_hbm, values_hbm, gain_hbm, decay_hbm, docs_hbm,
    out, keys, values, gain, decay, docs, arrival,
):
    heads, rows, width = keys.shape
    pairs = [(docs_hbm, docs), (decay_hbm, decay)]
    for h in range(heads):
        pairs += [(keys_hbm.at[h], keys.at[h]), (values_hbm.at[h], values.at[h])]
    pairs.append((gain_hbm, gain))
    copies = [pltpu.make_async_copy(a, b, arrival.at[i]) for i, (a, b) in enumerate(pairs)]
    for copy in copies:
        copy.start()
    lower = lower_mask(rows)
    base = heads * rows
    copies[0].wait()
    label_row = docs[...].astype(F32)
    label = as_columns(label_row, rows)[:, :1]
    last, first = label_row[:, rows - 1 :], label_row[:, :1]
    out[base + LAST : base + LAST + 1, :] = jnp.broadcast_to(last, (1, width))
    out[base + FIRST : base + FIRST + 1, :] = jnp.broadcast_to(first, (1, width))
    out[base + FIRST + 1 : base + EXTRA, :] = jnp.zeros((EXTRA - FIRST - 1, width), F32)
    copies[1].wait()
    weights = []
    for h in range(heads):
        cumulative = running(lower, decay[h : h + 1, :])
        total = cumulative[rows - 1 :, :]
        weights.append(jnp.where(label == last, jnp.exp(total - cumulative), 0.0))
        out[base + h : base + h + 1, :] = jnp.broadcast_to(total, (1, width))
    for h in range(heads):
        copies[2 + 2 * h].wait()
        copies[3 + 2 * h].wait()
        state = dot3(split(keys[h] * weights[h]), split(values[h]), TN)
        out[h * width : (h + 1) * width, :] = state
    for copy in copies[2 + 2 * heads :]:
        copy.wait()


def chip_meta(both, out, base, heads):
    width = out.shape[1]
    out[base : base + heads, :] = both[0, base : base + heads, :] + both[1, base : base + heads, :]
    out[base + LAST : base + LAST + 1, :] = both[1, base + LAST : base + LAST + 1, :]
    out[base + FIRST : base + FIRST + 1, :] = both[0, base + FIRST : base + FIRST + 1, :]
    out[base + FIRST + 1 : base + EXTRA, :] = jnp.zeros((EXTRA - FIRST - 1, width), F32)


def row_of(ref, which, at):
    return ref[which, at : at + 1, :]


def forward_join_body(heads, both, out):
    width = out.shape[1]
    base = heads * width
    linked = row_of(both, 0, base + LAST) == row_of(both, 1, base + LAST)
    for h in range(heads):
        weight = jnp.where(linked, jnp.exp(row_of(both, 1, base + h)), 0.0)
        at = slice(h * width, (h + 1) * width)
        out[at, :] = both[1, at, :] + weight * both[0, at, :]
    chip_meta(both, out, base, heads)


def scaled_place(asked, made, h, heads, each, rows):
    half = heads // 2
    return (asked, each + h * rows) if h < half else (made, each + (h - half) * rows)


def token_rows(asked, made, h, heads, rows):
    at = slice(h * rows, (h + 1) * rows)
    of, row = scaled_place(asked, made, h, heads, heads * rows, rows)
    return asked[at, :], made[at, :], of[row : row + rows, :]


def local_body(
    queries, keys, values, out_grad, gain, decay, docs, sent, asked, made, within, weighted
):
    del sent
    heads, rows, width = queries.shape
    each = heads * rows
    lower = lower_mask(rows)
    label_row = docs[...].astype(F32)
    allowed = lower & (as_columns(label_row, rows) == label_row)
    for h in range(heads):
        cumulative = running(lower, decay[h : h + 1, :])
        spread = cumulative - jnp.broadcast_to(cumulative, (rows, rows)).T
        weight = jnp.where(allowed, jnp.exp(jnp.where(allowed, spread, 0.0)), 0.0)
        both = weight * dot3(split(queries[h]), split(keys[h]), NT)
        within[h] = weight
        weighted[h] = both
        at = h * rows
        asked[at : at + rows, :] = queries[h]
        made[at : at + rows, :] = dot3(split(both), split(values[h]), NN)
        of, row = scaled_place(asked, made, h, heads, each, rows)
        of[row : row + rows, :] = gain[h : h + 1, :] * out_grad[h]
    meta = asked.shape[0] - EXTRA
    asked[meta : meta + heads, :] = decay[...]
    asked[meta + heads : meta + EXTRA, :] = jnp.broadcast_to(label_row, (EXTRA - heads, rows))


def pick(condition, one, other):
    return jnp.where(condition, one, other)


def link(near_row, far_row, total_row):
    return jnp.where(near_row == far_row, jnp.exp(total_row), 0.0)


def attended_body(core, asked, made, states, arrived, attended, priors, reaches, sums):
    _, heads, rows, width = attended.shape
    base = heads * width
    meta = asked.shape[1] - EXTRA
    lower = lower_mask(rows)
    second = core[0, 0] == 1
    near = row_of(arrived, 0, base + LAST)
    inner = row_of(states, 0, base + LAST)
    allowed = [
        as_columns(row_of(asked, c, meta + heads), rows) == label
        for c, label in enumerate((near, inner))
    ]
    squares = [jnp.zeros((rows, width), F32)] * 2
    inners = [jnp.zeros((rows, width), F32)] * 2
    for h in range(heads):
        at = slice(h * width, (h + 1) * width)
        far = link(near, row_of(arrived, 1, base + LAST), row_of(arrived, 0, base + h))
        outer_state = arrived[0, at, :] + far * arrived[1, at, :]
        passed = link(near, inner, row_of(states, 0, base + h))
        inner_state = states[0, at, :] + passed * outer_state
        priors[h] = pick(second, inner_state, outer_state)
        for c, state in enumerate((outer_state, inner_state)):
            queries, local, scaled = token_rows(asked.at[c], made.at[c], h, heads, rows)
            cumulative = running(lower, row_of(asked, c, meta + h))
            reach = jnp.where(allowed[c], jnp.exp(cumulative), 0.0)
            reaches[c, h] = reach
            value = local + reach * dot3(split(queries), split(state), NN)
            attended[c, h] = value
            squares[c] += value * value
            inners[c] += scaled * value
    for c in range(2):
        two = jnp.concatenate(
            [
                jnp.sum(squares[c].T, axis=0, keepdims=True),
                jnp.sum(inners[c].T, axis=0, keepdims=True),
            ],
            axis=0,
        )
        for i in range(sums.shape[0]):
            sums[i, :, c * rows : (c + 1) * rows] = two


def grad_state_body(width_all, sums, attended, asked, made, states, grad, out, back):
    _, heads, rows, width = attended.shape
    base = heads * width
    meta = asked.shape[1] - EXTRA
    total = jnp.sum(sums[...], axis=0)
    inverse_row = lax.rsqrt(total[0:1, :] / width_all + EPSILON)
    coupling_row = total[1:2, :] / width_all * inverse_row * inverse_row
    lower = lower_mask(rows)
    first_label = row_of(states, 0, base + FIRST)
    second_label = row_of(states, 1, base + FIRST)
    inverse = [as_columns(inverse_row[:, c * rows : (c + 1) * rows], rows) for c in range(2)]
    coupling = [as_columns(coupling_row[:, c * rows : (c + 1) * rows], rows) for c in range(2)]
    started = [
        as_columns(row_of(asked, c, meta + heads), rows) == label
        for c, label in enumerate((first_label, second_label))
    ]
    for h in range(heads):
        at = slice(h * width, (h + 1) * width)
        of_cores = []
        for c in range(2):
            queries, _, scaled = token_rows(asked.at[c], made.at[c], h, heads, rows)
            value = inverse[c] * (scaled - attended[c, h] * coupling[c])
            grad[c, h] = value
            cumulative = running(lower, row_of(asked, c, meta + h))
            reach = jnp.where(started[c], jnp.exp(cumulative), 0.0)
            of_cores.append(dot3(split(queries * reach), split(value), TN))
        back[at, :] = of_cores[1]
        passed = link(first_label, second_label, row_of(states, 0, base + h))
        out[at, :] = of_cores[0] + passed * of_cores[1]
    chip_meta(states, out, base, heads)


def main_grad_body(
    core, queries, keys, values, decay, within, weighted, grad, prior, from_prior, sent,
    query_grad, key_local, value_local, tails, *halves,
):
    del sent
    lower = lower_mask(queries.shape[1])
    for h in range(queries.shape[0]):
        of_grad = split(grad[core[0, 0], h])
        of_keys = split(keys[h])
        of_values = split(values[h])
        of_both = split(within[h] * dot3(of_grad, of_values, NT))
        query_grad[h] = dot3(of_both, of_keys, NN) + from_prior[core[0, 0], h] * dot3(of_grad, split(prior[h]), NT)
        key_local[h] = dot3(of_both, split(queries[h]), TN)
        value_local[h] = dot3(split(weighted[h]), of_grad, TN)
        for half, part in zip(halves, (*of_keys, *of_values)):
            half[h] = part
        cumulative = running(lower, decay[h : h + 1, :])
        tail = jnp.exp(cumulative[queries.shape[1] - 1 :, :] - cumulative)
        tails[h] = jnp.broadcast_to(tail, tails.shape[1:])


def last_grad_body(
    core, keys_high, keys_low, values_high, values_low, tails, docs, key_local, value_local,
    meta, back, arrived, key_grad_hbm, value_grad_hbm, key_grad, value_grad, sent,
):
    heads, rows, width = tails.shape
    base = heads * width
    first = core[0, 0] == 0
    near = row_of(arrived, 0, base + FIRST)
    chained = near == row_of(arrived, 1, base + FIRST)
    inner = row_of(meta, 1, base + FIRST)
    linked = inner == near
    ahead = as_columns(docs[...].astype(F32), rows) == jnp.where(first, inner, near)
    copies = []
    for h in range(heads):
        at = slice(h * width, (h + 1) * width)
        weight = jnp.where(chained, jnp.exp(row_of(arrived, 0, base + h)), 0.0)
        state = arrived[0, at, :] + weight * arrived[1, at, :]
        passed = jnp.where(linked, jnp.exp(row_of(meta, 1, base + h)), 0.0)
        of_state = split(jnp.where(first, back[at, :] + passed * state, state))
        to_next = jnp.where(ahead, tails[h], 0.0)
        key_grad[h] = key_local[h] + to_next * dot3((values_high[h], values_low[h]), of_state, NT)
        value_grad[h] = value_local[h] + to_next * dot3((keys_high[h], keys_low[h]), of_state, NN)
        for i, (a, b) in enumerate(((key_grad, key_grad_hbm), (value_grad, value_grad_hbm))):
            copies.append(pltpu.make_async_copy(a.at[h], b.at[h], sent.at[2 * h + i]))
            copies[-1].start()
    for copy in copies:
        copy.wait()


def per_device(queries, keys, values, out_grad, norm_gain, log_decay, doc_ids):
    heads, rows, width = queries.shape
    seq = lax.axis_size("chip") * 2
    group = lax.axis_size("head")
    docs = doc_ids.reshape(1, rows)
    core = lax.axis_index("core").astype(jnp.int32).reshape(1, 1)
    shape = lambda *dims: jax.ShapeDtypeStruct(dims, F32)
    block = shape(heads, rows, width)
    payload = shape(heads * width + EXTRA, width)
    product = 6 * heads * rows * width * width

    given = [keys, values, norm_gain, log_decay, docs]
    own, keys, values, norm_gain, log_decay, docs = kernel_call(
        state_body,
        (payload, *(jax.ShapeDtypeStruct(a.shape, a.dtype) for a in given)),
        product,
        "h" * len(given),
        scratch=(pltpu.SemaphoreType.DMA((2 * heads + 3,)),),
    )(*(pltpu.with_memory_space_constraint(a, pltpu.HBM) for a in given))
    states = lax.all_gather(own, "core")
    chip_state = kernel_call(functools.partial(forward_join_body, heads), payload, product // 64)(states)
    ahead = [(i, i + 2 + 2 * (i % 2)) for i in range(seq)]
    moved = lax.ppermute(chip_state, ("chip", "core"), [(a, b) for a, b in ahead if b < seq])
    more = heads // 2 * rows
    asked, made, within, weighted = kernel_call(
        local_body,
        (
            shape(heads * rows + more + EXTRA, width),
            shape(2 * heads * rows - more, width),
            block,
            block,
        ),
        2 * product,
    )(queries, keys, values, out_grad, norm_gain, log_decay, docs, chip_state)
    asked = lax.all_gather(asked, "core")
    made, asked = lax.optimization_barrier((made, asked))
    made = lax.all_gather(made, "core")
    moved, made = lax.optimization_barrier((moved, made))
    arrived = lax.all_gather(moved, "core")
    twice = shape(2, heads, rows, width)
    attended, prior, from_prior, sums = kernel_call(
        attended_body, (twice, block, twice, shape(group, 2, 2 * rows)), 2 * product, "s"
    )(core, asked, made, states, arrived)
    sums = lax.all_to_all(sums, "head", 0, 0, tiled=True)
    grad, chip_back, back = kernel_call(
        functools.partial(grad_state_body, heads * width * group),
        (twice, payload, shape(heads * width, width)),
        2 * product,
    )(sums, attended, asked, made, states)
    behind = [(i, i - 2 - 2 * (i % 2)) for i in range(seq)]
    moved_back = lax.ppermute(chip_back, ("chip", "core"), [(a, b) for a, b in behind if b >= 0])
    half = jax.ShapeDtypeStruct((heads, rows, width), BF16)
    query_grad, key_local, value_local, tails, *halves = kernel_call(
        main_grad_body, (block,) * 4 + (half,) * 4, 5 * product, "s"
    )(
        core, queries, keys, values, log_decay, within, weighted, grad, prior, from_prior, chip_back
    )
    arrived_back = lax.all_gather(moved_back, "core")
    held = pltpu.VMEM((heads, rows, width), F32)
    key_grad, value_grad = kernel_call(
        last_grad_body,
        (block,) * 2,
        2 * product,
        "s",
        "hh",
        (held, held, pltpu.SemaphoreType.DMA((2 * heads,))),
    )(core, *halves, tails, docs, key_local, value_local, states, back, arrived_back)
    return query_grad, key_grad, value_grad


def solution(mesh):
    seq, head = mesh.devices.shape
    fine = Mesh(mesh.devices.reshape(seq // 2, 2, head), ("chip", "core", "head"))
    tokens = ("chip", "core")
    block = P("head", tokens, None)
    return jax.shard_map(
        per_device,
        mesh=fine,
        in_specs=(block, block, block, block, P("head", None), P("head", tokens), P(tokens)),
        out_specs=(block, block, block),
        check_vma=False,
    )
```

```python
import functools

import jax
import jax.numpy as jnp
from jax import lax
from jax.experimental import pallas as pl
from jax.experimental.pallas import tpu as pltpu
from jax.sharding import Mesh
from jax.sharding import PartitionSpec as P

EPSILON = 1e-06
F32 = jnp.float32
BF16 = jnp.bfloat16
NN = (((1,), (0,)), ((), ()))
NT = (((1,), (1,)), ((), ()))
TN = (((0,), (0,)), ((), ()))
VMEM_LIMIT = 12 * 2**20
LAST, FIRST, EXTRA = 4, 5, 8


def split(x):
    high = x.astype(BF16)
    return high, (x - high.astype(F32)).astype(BF16)


def dot3(left, right, dims):
    one = functools.partial(lax.dot_general, dimension_numbers=dims, preferred_element_type=F32)
    return one(left[0], right[0]) + (one(left[0], right[1]) + one(left[1], right[0]))


def kernel_call(body, outs, flops, kinds="", out_kinds="", scratch=()):
    spaces = {"h": pltpu.HBM, "s": pltpu.SMEM, "v": pltpu.VMEM}

    def call(*operands):
        of = [pl.BlockSpec(memory_space=spaces[c]) for c in kinds.ljust(len(operands), "v")]
        more = {}
        if out_kinds:
            made = [pl.BlockSpec(memory_space=spaces[c]) for c in out_kinds]
            more["out_specs"] = tuple(made)
        return pl.pallas_call(
            body,
            out_shape=outs,
            in_specs=of,
            scratch_shapes=list(scratch),
            compiler_params=pltpu.CompilerParams(vmem_limit_bytes=VMEM_LIMIT),
            cost_estimate=pl.CostEstimate(flops=flops, bytes_accessed=2**20, transcendentals=0),
            **more,
        )(*operands)

    return call


def as_columns(row, rows):
    return jnp.broadcast_to(row, (rows, row.shape[1])).T


def lower_mask(rows):
    return lax.broadcasted_iota(jnp.int32, (rows, rows), 0) >= lax.broadcasted_iota(
        jnp.int32, (rows, rows), 1
    )


def running(lower, decay_row):
    return jnp.sum(jnp.where(lower, decay_row, 0.0), axis=1, keepdims=True)


def state_body(
    keys_hbm, values_hbm, gain_hbm, decay_hbm, docs_hbm,
    out, keys, values, gain, decay, docs, arrival,
):
    heads, rows, width = keys.shape
    pairs = [
        (docs_hbm, docs), (decay_hbm, decay), (keys_hbm, keys), (values_hbm, values), (gain_hbm, gain),
    ]
    copies = [pltpu.make_async_copy(a, b, arrival.at[i]) for i, (a, b) in enumerate(pairs)]
    for copy in copies:
        copy.start()
    lower = lower_mask(rows)
    base = heads * rows
    copies[0].wait()
    label_row = docs[...].astype(F32)
    label = as_columns(label_row, rows)[:, :1]
    last, first = label_row[:, rows - 1 :], label_row[:, :1]
    out[base + LAST : base + LAST + 1, :] = jnp.broadcast_to(last, (1, width))
    out[base + FIRST : base + FIRST + 1, :] = jnp.broadcast_to(first, (1, width))
    out[base + FIRST + 1 : base + EXTRA, :] = jnp.zeros((EXTRA - FIRST - 1, width), F32)
    copies[1].wait()
    weights = []
    for h in range(heads):
        cumulative = running(lower, decay[h : h + 1, :])
        total = cumulative[rows - 1 :, :]
        weights.append(jnp.where(label == last, jnp.exp(total - cumulative), 0.0))
        out[base + h : base + h + 1, :] = jnp.broadcast_to(total, (1, width))
    for copy in copies[2:]:
        copy.wait()
    for h in range(heads):
        state = dot3(split(keys[h] * weights[h]), split(values[h]), TN)
        out[h * width : (h + 1) * width, :] = state


def chip_meta(both, out, base, heads):
    width = out.shape[1]
    out[base : base + heads, :] = both[0, base : base + heads, :] + both[1, base : base + heads, :]
    out[base + LAST : base + LAST + 1, :] = both[1, base + LAST : base + LAST + 1, :]
    out[base + FIRST : base + FIRST + 1, :] = both[0, base + FIRST : base + FIRST + 1, :]
    out[base + FIRST + 1 : base + EXTRA, :] = jnp.zeros((EXTRA - FIRST - 1, width), F32)


def row_of(ref, which, at):
    return ref[which, at : at + 1, :]


def forward_join_body(heads, both, out):
    width = out.shape[1]
    base = heads * width
    linked = row_of(both, 0, base + LAST) == row_of(both, 1, base + LAST)
    for h in range(heads):
        weight = jnp.where(linked, jnp.exp(row_of(both, 1, base + h)), 0.0)
        at = slice(h * width, (h + 1) * width)
        out[at, :] = both[1, at, :] + weight * both[0, at, :]
    chip_meta(both, out, base, heads)


def scaled_place(asked, made, h, heads, each, rows):
    half = heads // 2
    return (asked, each + h * rows) if h < half else (made, each + (h - half) * rows)


def token_rows(asked, made, h, heads, rows):
    at = slice(h * rows, (h + 1) * rows)
    of, row = scaled_place(asked, made, h, heads, heads * rows, rows)
    return asked[at, :], made[at, :], of[row : row + rows, :]


def local_body(
    queries, keys, values, out_grad, gain, decay, docs, sent, asked, made, within, weighted
):
    del sent
    heads, rows, width = queries.shape
    each = heads * rows
    lower = lower_mask(rows)
    label_row = docs[...].astype(F32)
    allowed = lower & (as_columns(label_row, rows) == label_row)
    for h in range(heads):
        cumulative = running(lower, decay[h : h + 1, :])
        spread = cumulative - jnp.broadcast_to(cumulative, (rows, rows)).T
        weight = jnp.where(allowed, jnp.exp(jnp.where(allowed, spread, 0.0)), 0.0)
        both = weight * dot3(split(queries[h]), split(keys[h]), NT)
        within[h] = weight
        weighted[h] = both
        at = h * rows
        asked[at : at + rows, :] = queries[h]
        made[at : at + rows, :] = dot3(split(both), split(values[h]), NN)
        of, row = scaled_place(asked, made, h, heads, each, rows)
        of[row : row + rows, :] = gain[h : h + 1, :] * out_grad[h]
    meta = asked.shape[0] - EXTRA
    asked[meta : meta + heads, :] = decay[...]
    asked[meta + heads : meta + EXTRA, :] = jnp.broadcast_to(label_row, (EXTRA - heads, rows))


def pick(condition, one, other):
    return jnp.where(condition, one, other)


def link(near_row, far_row, total_row):
    return jnp.where(near_row == far_row, jnp.exp(total_row), 0.0)


def prepare_body(asked, states, high, low, start_high, start_low, passes):
    _, heads, rows, width = high.shape
    base = heads * width
    meta = asked.shape[1] - EXTRA
    lower = lower_mask(rows)
    for c in range(2):
        label = as_columns(row_of(asked, c, meta + heads), rows)
        started = label == row_of(states, c, base + FIRST)
        for h in range(heads):
            queries = asked[c, h * rows : (h + 1) * rows, :]
            high[c, h], low[c, h] = split(queries)
            decay = jnp.exp(running(lower, row_of(asked, c, meta + h)))
            passes[c, h] = jnp.broadcast_to(decay, (rows, width))
            start_high[c, h], start_low[c, h] = split((queries * jnp.where(started, decay, 0.0)).T)


def attended_body(
    core, asked, made, states, high, low, passes, arrived, attended, priors, reaches, sums
):
    _, heads, rows, width = attended.shape
    base = heads * width
    meta = asked.shape[1] - EXTRA
    second = core[0, 0] == 1
    near = row_of(arrived, 0, base + LAST)
    inner = row_of(states, 0, base + LAST)
    allowed = [
        as_columns(row_of(asked, c, meta + heads), rows) == label
        for c, label in enumerate((near, inner))
    ]
    squares = [jnp.zeros((rows, width), F32)] * 2
    inners = [jnp.zeros((rows, width), F32)] * 2
    for h in range(heads):
        at = slice(h * width, (h + 1) * width)
        far = link(near, row_of(arrived, 1, base + LAST), row_of(arrived, 0, base + h))
        outer_state = arrived[0, at, :] + far * arrived[1, at, :]
        passed = link(near, inner, row_of(states, 0, base + h))
        inner_state = states[0, at, :] + passed * outer_state
        priors[h] = pick(second, inner_state, outer_state)
        for c, state in enumerate((outer_state, inner_state)):
            _, local, scaled = token_rows(asked.at[c], made.at[c], h, heads, rows)
            reach = jnp.where(allowed[c], passes[c, h], 0.0)
            reaches[c, h] = reach
            value = local + reach * dot3((high[c, h], low[c, h]), split(state), NN)
            attended[c, h] = value
            squares[c] += value * value
            inners[c] += scaled * value
    for c in range(2):
        two = jnp.concatenate(
            [
                jnp.sum(squares[c].T, axis=0, keepdims=True),
                jnp.sum(inners[c].T, axis=0, keepdims=True),
            ],
            axis=0,
        )
        for i in range(sums.shape[0]):
            sums[i, :, c * rows : (c + 1) * rows] = two


def grad_state_body(
    width_all, sums, attended, asked, made, states, start_high, start_low, grad, out, back
):
    _, heads, rows, width = attended.shape
    base = heads * width
    total = jnp.sum(sums[...], axis=0)
    inverse_row = lax.rsqrt(total[0:1, :] / width_all + EPSILON)
    coupling_row = total[1:2, :] / width_all * inverse_row * inverse_row
    first_label = row_of(states, 0, base + FIRST)
    second_label = row_of(states, 1, base + FIRST)
    inverse = [as_columns(inverse_row[:, c * rows : (c + 1) * rows], rows) for c in range(2)]
    coupling = [as_columns(coupling_row[:, c * rows : (c + 1) * rows], rows) for c in range(2)]
    for h in range(heads):
        at = slice(h * width, (h + 1) * width)
        of_cores = []
        for c in range(2):
            _, _, scaled = token_rows(asked.at[c], made.at[c], h, heads, rows)
            value = inverse[c] * (scaled - attended[c, h] * coupling[c])
            grad[c, h] = value
            of_cores.append(dot3((start_high[c, h], start_low[c, h]), split(value), NN))
        back[at, :] = of_cores[1]
        passed = link(first_label, second_label, row_of(states, 0, base + h))
        out[at, :] = of_cores[0] + passed * of_cores[1]
    chip_meta(states, out, base, heads)


def main_grad_body(
    core, queries, keys, values, decay, within, weighted, grad, prior, from_prior, sent,
    query_grad, key_local, value_local, tails, *halves,
):
    del sent
    lower = lower_mask(queries.shape[1])
    for h in range(queries.shape[0]):
        of_grad = split(grad[core[0, 0], h])
        of_keys = split(keys[h])
        of_values = split(values[h])
        of_both = split(within[h] * dot3(of_grad, of_values, NT))
        query_grad[h] = dot3(of_both, of_keys, NN) + from_prior[core[0, 0], h] * dot3(of_grad, split(prior[h]), NT)
        key_local[h] = dot3(of_both, split(queries[h]), TN)
        value_local[h] = dot3(split(weighted[h]), of_grad, TN)
        for half, part in zip(halves, (*of_keys, *of_values)):
            half[h] = part
        cumulative = running(lower, decay[h : h + 1, :])
        tail = jnp.exp(cumulative[queries.shape[1] - 1 :, :] - cumulative)
        tails[h] = jnp.broadcast_to(tail, tails.shape[1:])


def last_grad_body(
    core, keys_high, keys_low, values_high, values_low, tails, docs, key_local, value_local,
    meta, back, arrived, key_grad_hbm, value_grad_hbm, key_grad, value_grad, sent,
):
    heads, rows, width = tails.shape
    base = heads * width
    first = core[0, 0] == 0
    near = row_of(arrived, 0, base + FIRST)
    chained = near == row_of(arrived, 1, base + FIRST)
    inner = row_of(meta, 1, base + FIRST)
    linked = inner == near
    ahead = as_columns(docs[...].astype(F32), rows) == jnp.where(first, inner, near)
    copies = []
    for h in range(heads):
        at = slice(h * width, (h + 1) * width)
        weight = jnp.where(chained, jnp.exp(row_of(arrived, 0, base + h)), 0.0)
        state = arrived[0, at, :] + weight * arrived[1, at, :]
        passed = jnp.where(linked, jnp.exp(row_of(meta, 1, base + h)), 0.0)
        of_state = split(jnp.where(first, back[at, :] + passed * state, state))
        to_next = jnp.where(ahead, tails[h], 0.0)
        key_grad[h] = key_local[h] + to_next * dot3((values_high[h], values_low[h]), of_state, NT)
        value_grad[h] = value_local[h] + to_next * dot3((keys_high[h], keys_low[h]), of_state, NN)
        for i, (a, b) in enumerate(((key_grad, key_grad_hbm), (value_grad, value_grad_hbm))):
            copies.append(pltpu.make_async_copy(a.at[h], b.at[h], sent.at[2 * h + i]))
            copies[-1].start()
    for copy in copies:
        copy.wait()


def per_device(queries, keys, values, out_grad, norm_gain, log_decay, doc_ids):
    heads, rows, width = queries.shape
    seq = lax.axis_size("chip") * 2
    group = lax.axis_size("head")
    docs = doc_ids.reshape(1, rows)
    core = lax.axis_index("core").astype(jnp.int32).reshape(1, 1)
    shape = lambda *dims: jax.ShapeDtypeStruct(dims, F32)
    block = shape(heads, rows, width)
    payload = shape(heads * width + EXTRA, width)
    product = 6 * heads * rows * width * width

    given = [keys, values, norm_gain, log_decay, docs]
    own, keys, values, norm_gain, log_decay, docs = kernel_call(
        state_body,
        (payload, *(jax.ShapeDtypeStruct(a.shape, a.dtype) for a in given)),
        product,
        "h" * len(given),
        scratch=(pltpu.SemaphoreType.DMA((len(given),)),),
    )(*(pltpu.with_memory_space_constraint(a, pltpu.HBM) for a in given))
    states = lax.all_gather(own, "core")
    chip_state = kernel_call(functools.partial(forward_join_body, heads), payload, product // 64)(states)
    ahead = [(i, i + 2 + 2 * (i % 2)) for i in range(seq)]
    moved = lax.ppermute(chip_state, ("chip", "core"), [(a, b) for a, b in ahead if b < seq])
    more = heads // 2 * rows
    asked, made, within, weighted = kernel_call(
        local_body,
        (
            shape(heads * rows + more + EXTRA, width),
            shape(2 * heads * rows - more, width),
            block,
            block,
        ),
        2 * product,
    )(queries, keys, values, out_grad, norm_gain, log_decay, docs, chip_state)
    asked = lax.all_gather(asked, "core")
    made, asked = lax.optimization_barrier((made, asked))
    made = lax.all_gather(made, "core")
    twice = shape(2, heads, rows, width)
    halves_twice = jax.ShapeDtypeStruct(twice.shape, BF16)
    high, low, start_high, start_low, passes = kernel_call(
        prepare_body, (halves_twice,) * 4 + (twice,), product // 4
    )(asked, states)
    moved, made, passes = lax.optimization_barrier((moved, made, passes))
    arrived = lax.all_gather(moved, "core")
    attended, prior, from_prior, sums = kernel_call(
        attended_body, (twice, block, twice, shape(group, 2, 2 * rows)), 2 * product, "s"
    )(core, asked, made, states, high, low, passes, arrived)
    sums = lax.all_to_all(sums, "head", 0, 0, tiled=True)
    grad, chip_back, back = kernel_call(
        functools.partial(grad_state_body, heads * width * group),
        (twice, payload, shape(heads * width, width)),
        2 * product,
    )(sums, attended, asked, made, states, start_high, start_low)
    behind = [(i, i - 2 - 2 * (i % 2)) for i in range(seq)]
    moved_back = lax.ppermute(chip_back, ("chip", "core"), [(a, b) for a, b in behind if b >= 0])
    half = jax.ShapeDtypeStruct((heads, rows, width), BF16)
    query_grad, key_local, value_local, tails, *halves = kernel_call(
        main_grad_body, (block,) * 4 + (half,) * 4, 5 * product, "s"
    )(
        core, queries, keys, values, log_decay, within, weighted, grad, prior, from_prior, chip_back
    )
    arrived_back = lax.all_gather(moved_back, "core")
    held = pltpu.VMEM((heads, rows, width), F32)
    key_grad, value_grad = kernel_call(
        last_grad_body,
        (block,) * 2,
        2 * product,
        "s",
        "hh",
        (held, held, pltpu.SemaphoreType.DMA((2 * heads,))),
    )(core, *halves, tails, docs, key_local, value_local, states, back, arrived_back)
    return query_grad, key_grad, value_grad


def solution(mesh):
    seq, head = mesh.devices.shape
    fine = Mesh(mesh.devices.reshape(seq // 2, 2, head), ("chip", "core", "head"))
    tokens = ("chip", "core")
    block = P("head", tokens, None)
    return jax.shard_map(
        per_device,
        mesh=fine,
        in_specs=(block, block, block, block, P("head", None), P("head", tokens), P(tokens)),
        out_specs=(block, block, block),
        check_vma=False,
    )
```

```python
import functools

import jax
import jax.numpy as jnp
from jax import lax
from jax.experimental import pallas as pl
from jax.experimental.pallas import tpu as pltpu
from jax.sharding import Mesh
from jax.sharding import PartitionSpec as P

EPSILON = 1e-06
F32 = jnp.float32
BF16 = jnp.bfloat16
NN = (((1,), (0,)), ((), ()))
NT = (((1,), (1,)), ((), ()))
TN = (((0,), (0,)), ((), ()))
VMEM_LIMIT = 12 * 2**20
LAST, FIRST, EXTRA = 4, 5, 8


def split(x):
    high = x.astype(BF16)
    return high, (x - high.astype(F32)).astype(BF16)


def dot3(left, right, dims):
    one = functools.partial(lax.dot_general, dimension_numbers=dims, preferred_element_type=F32)
    return one(left[0], right[0]) + (one(left[0], right[1]) + one(left[1], right[0]))


def kernel_call(body, outs, flops, kinds="", out_kinds="", scratch=()):
    spaces = {"h": pltpu.HBM, "s": pltpu.SMEM, "v": pltpu.VMEM}

    def call(*operands):
        of = [pl.BlockSpec(memory_space=spaces[c]) for c in kinds.ljust(len(operands), "v")]
        more = {}
        if out_kinds:
            made = [pl.BlockSpec(memory_space=spaces[c]) for c in out_kinds]
            more["out_specs"] = tuple(made)
        return pl.pallas_call(
            body,
            out_shape=outs,
            in_specs=of,
            scratch_shapes=list(scratch),
            compiler_params=pltpu.CompilerParams(vmem_limit_bytes=VMEM_LIMIT),
            cost_estimate=pl.CostEstimate(flops=flops, bytes_accessed=2**20, transcendentals=0),
            **more,
        )(*operands)

    return call


def as_columns(row, rows):
    return jnp.broadcast_to(row, (rows, row.shape[1])).T


def lower_mask(rows):
    return lax.broadcasted_iota(jnp.int32, (rows, rows), 0) >= lax.broadcasted_iota(
        jnp.int32, (rows, rows), 1
    )


def running(lower, decay_row):
    return jnp.sum(jnp.where(lower, decay_row, 0.0), axis=1, keepdims=True)


def state_body(
    keys_hbm, values_hbm, gain_hbm, decay_hbm, docs_hbm,
    out, keys, values, gain, decay, docs, arrival,
):
    heads, rows, width = keys.shape
    pairs = [
        (docs_hbm, docs), (decay_hbm, decay), (keys_hbm, keys), (values_hbm, values), (gain_hbm, gain),
    ]
    copies = [pltpu.make_async_copy(a, b, arrival.at[i]) for i, (a, b) in enumerate(pairs)]
    for copy in copies:
        copy.start()
    lower = lower_mask(rows)
    base = heads * rows
    copies[0].wait()
    label_row = docs[...].astype(F32)
    label = as_columns(label_row, rows)[:, :1]
    last, first = label_row[:, rows - 1 :], label_row[:, :1]
    out[base + LAST : base + LAST + 1, :] = jnp.broadcast_to(last, (1, width))
    out[base + FIRST : base + FIRST + 1, :] = jnp.broadcast_to(first, (1, width))
    out[base + FIRST + 1 : base + EXTRA, :] = jnp.zeros((EXTRA - FIRST - 1, width), F32)
    copies[1].wait()
    weights = []
    for h in range(heads):
        cumulative = running(lower, decay[h : h + 1, :])
        total = cumulative[rows - 1 :, :]
        weights.append(jnp.where(label == last, jnp.exp(total - cumulative), 0.0))
        out[base + h : base + h + 1, :] = jnp.broadcast_to(total, (1, width))
    for copy in copies[2:]:
        copy.wait()
    for h in range(heads):
        state = dot3(split(keys[h] * weights[h]), split(values[h]), TN)
        out[h * width : (h + 1) * width, :] = state


def chip_meta(both, out, base, heads):
    width = out.shape[1]
    out[base : base + heads, :] = both[0, base : base + heads, :] + both[1, base : base + heads, :]
    out[base + LAST : base + LAST + 1, :] = both[1, base + LAST : base + LAST + 1, :]
    out[base + FIRST : base + FIRST + 1, :] = both[0, base + FIRST : base + FIRST + 1, :]
    out[base + FIRST + 1 : base + EXTRA, :] = jnp.zeros((EXTRA - FIRST - 1, width), F32)


def row_of(ref, which, at):
    return ref[which, at : at + 1, :]


def forward_join_body(heads, both, out):
    width = out.shape[1]
    base = heads * width
    linked = row_of(both, 0, base + LAST) == row_of(both, 1, base + LAST)
    for h in range(heads):
        weight = jnp.where(linked, jnp.exp(row_of(both, 1, base + h)), 0.0)
        at = slice(h * width, (h + 1) * width)
        out[at, :] = both[1, at, :] + weight * both[0, at, :]
    chip_meta(both, out, base, heads)


def scaled_place(asked, made, h, heads, each, rows):
    half = heads // 2
    return (asked, each + h * rows) if h < half else (made, each + (h - half) * rows)


def token_rows(asked, made, h, heads, rows):
    at = slice(h * rows, (h + 1) * rows)
    of, row = scaled_place(asked, made, h, heads, heads * rows, rows)
    return asked[at, :], made[at, :], of[row : row + rows, :]


def local_body(
    queries, keys, values, out_grad, gain, decay, docs, sent, asked, made, within, weighted
):
    del sent
    heads, rows, width = queries.shape
    each = heads * rows
    lower = lower_mask(rows)
    label_row = docs[...].astype(F32)
    allowed = lower & (as_columns(label_row, rows) == label_row)
    for h in range(heads):
        cumulative = running(lower, decay[h : h + 1, :])
        spread = cumulative - jnp.broadcast_to(cumulative, (rows, rows)).T
        weight = jnp.where(allowed, jnp.exp(jnp.where(allowed, spread, 0.0)), 0.0)
        both = weight * dot3(split(queries[h]), split(keys[h]), NT)
        within[h] = weight
        weighted[h] = both
        at = h * rows
        asked[at : at + rows, :] = queries[h]
        made[at : at + rows, :] = dot3(split(both), split(values[h]), NN)
        of, row = scaled_place(asked, made, h, heads, each, rows)
        of[row : row + rows, :] = gain[h : h + 1, :] * out_grad[h]
    meta = asked.shape[0] - EXTRA
    asked[meta : meta + heads, :] = decay[...]
    asked[meta + heads : meta + EXTRA, :] = jnp.broadcast_to(label_row, (EXTRA - heads, rows))


def pick(condition, one, other):
    return jnp.where(condition, one, other)


def link(near_row, far_row, total_row):
    return jnp.where(near_row == far_row, jnp.exp(total_row), 0.0)


def states_ahead(states, arrived, h, width):
    base = arrived.shape[1] - EXTRA
    at = slice(h * width, (h + 1) * width)
    near = row_of(arrived, 0, base + LAST)
    inner = row_of(states, 0, base + LAST)
    far = link(near, row_of(arrived, 1, base + LAST), row_of(arrived, 0, base + h))
    outer_state = arrived[0, at, :] + far * arrived[1, at, :]
    passed = link(near, inner, row_of(states, 0, base + h))
    return outer_state, states[0, at, :] + passed * outer_state


def prepare_body(asked, states, high, low, start_high, start_low, passes):
    _, heads, rows, width = high.shape
    base = heads * width
    meta = asked.shape[1] - EXTRA
    lower = lower_mask(rows)
    for c in range(2):
        label = as_columns(row_of(asked, c, meta + heads), rows)
        started = label == row_of(states, c, base + FIRST)
        for h in range(heads):
            queries = asked[c, h * rows : (h + 1) * rows, :]
            high[c, h], low[c, h] = split(queries)
            decay = jnp.exp(running(lower, row_of(asked, c, meta + h)))
            passes[c, h] = jnp.broadcast_to(decay, (rows, width))
            start_high[c, h], start_low[c, h] = split((queries * jnp.where(started, decay, 0.0)).T)


def attended_body(
    asked, made, states, high, low, passes, arrived, attended, sums
):
    _, heads, rows, width = attended.shape
    base = heads * width
    meta = asked.shape[1] - EXTRA
    near = row_of(arrived, 0, base + LAST)
    inner = row_of(states, 0, base + LAST)
    allowed = [
        as_columns(row_of(asked, c, meta + heads), rows) == label
        for c, label in enumerate((near, inner))
    ]
    squares = [jnp.zeros((rows, width), F32)] * 2
    inners = [jnp.zeros((rows, width), F32)] * 2
    for h in range(heads):
        for c, state in enumerate(states_ahead(states, arrived, h, width)):
            _, local, scaled = token_rows(asked.at[c], made.at[c], h, heads, rows)
            reach = jnp.where(allowed[c], passes[c, h], 0.0)
            value = local + reach * dot3((high[c, h], low[c, h]), split(state), NN)
            attended[c, h] = value
            squares[c] += value * value
            inners[c] += scaled * value
    for c in range(2):
        two = jnp.concatenate(
            [
                jnp.sum(squares[c].T, axis=0, keepdims=True),
                jnp.sum(inners[c].T, axis=0, keepdims=True),
            ],
            axis=0,
        )
        for i in range(sums.shape[0]):
            sums[i, :, c * rows : (c + 1) * rows] = two


def grad_state_body(
    width_all, sums, attended, asked, made, states, start_high, start_low, grad, out, back
):
    _, heads, rows, width = attended.shape
    base = heads * width
    total = jnp.sum(sums[...], axis=0)
    inverse_row = lax.rsqrt(total[0:1, :] / width_all + EPSILON)
    coupling_row = total[1:2, :] / width_all * inverse_row * inverse_row
    first_label = row_of(states, 0, base + FIRST)
    second_label = row_of(states, 1, base + FIRST)
    inverse = [as_columns(inverse_row[:, c * rows : (c + 1) * rows], rows) for c in range(2)]
    coupling = [as_columns(coupling_row[:, c * rows : (c + 1) * rows], rows) for c in range(2)]
    for h in range(heads):
        at = slice(h * width, (h + 1) * width)
        of_cores = []
        for c in range(2):
            _, _, scaled = token_rows(asked.at[c], made.at[c], h, heads, rows)
            value = inverse[c] * (scaled - attended[c, h] * coupling[c])
            grad[c, h] = value
            of_cores.append(dot3((start_high[c, h], start_low[c, h]), split(value), NN))
        back[at, :] = of_cores[1]
        passed = link(first_label, second_label, row_of(states, 0, base + h))
        out[at, :] = of_cores[0] + passed * of_cores[1]
    chip_meta(states, out, base, heads)


def main_grad_body(
    queries, keys, values, decay, docs, within, weighted, grad, states, arrived, sent,
    query_grad, key_local, value_local, tails, *halves,
):
    del sent
    rows, width = queries.shape[1:]
    base = arrived.shape[1] - EXTRA
    lower = lower_mask(rows)
    second = lax.axis_index("core") == 1
    near = pick(second, row_of(states, 0, base + LAST), row_of(arrived, 0, base + LAST))
    ahead = as_columns(docs[...].astype(F32), rows) == near
    for h in range(queries.shape[0]):
        of_grad = split(grad[lax.axis_index("core"), h])
        of_keys = split(keys[h])
        of_values = split(values[h])
        of_both = split(within[h] * dot3(of_grad, of_values, NT))
        cumulative = running(lower, decay[h : h + 1, :])
        outer_state, inner_state = states_ahead(states, arrived, h, width)
        of_state = split(pick(second, inner_state, outer_state))
        reach = jnp.where(ahead, jnp.exp(cumulative), 0.0)
        query_grad[h] = dot3(of_both, of_keys, NN) + reach * dot3(of_grad, of_state, NT)
        key_local[h] = dot3(of_both, split(queries[h]), TN)
        value_local[h] = dot3(split(weighted[h]), of_grad, TN)
        for half, part in zip(halves, (*of_keys, *of_values)):
            half[h] = part
        tail = jnp.exp(cumulative[rows - 1 :, :] - cumulative)
        tails[h] = jnp.broadcast_to(tail, tails.shape[1:])


def last_grad_body(
    keys_high, keys_low, values_high, values_low, tails, docs, key_local, value_local,
    meta, back, arrived, key_grad_hbm, value_grad_hbm, key_grad, value_grad, sent,
):
    heads, rows, width = tails.shape
    base = heads * width
    first = lax.axis_index("core") == 0
    near = row_of(arrived, 0, base + FIRST)
    chained = near == row_of(arrived, 1, base + FIRST)
    inner = row_of(meta, 1, base + FIRST)
    linked = inner == near
    ahead = as_columns(docs[...].astype(F32), rows) == jnp.where(first, inner, near)
    copies = []
    for h in range(heads):
        at = slice(h * width, (h + 1) * width)
        weight = jnp.where(chained, jnp.exp(row_of(arrived, 0, base + h)), 0.0)
        state = arrived[0, at, :] + weight * arrived[1, at, :]
        passed = jnp.where(linked, jnp.exp(row_of(meta, 1, base + h)), 0.0)
        of_state = split(jnp.where(first, back[at, :] + passed * state, state))
        to_next = jnp.where(ahead, tails[h], 0.0)
        key_grad[h] = key_local[h] + to_next * dot3((values_high[h], values_low[h]), of_state, NT)
        value_grad[h] = value_local[h] + to_next * dot3((keys_high[h], keys_low[h]), of_state, NN)
        if h % 2 == 0:
            continue
        for i, (a, b) in enumerate(((key_grad, key_grad_hbm), (value_grad, value_grad_hbm))):
            done = slice(h - 1, h + 1)
            copies.append(pltpu.make_async_copy(a.at[done], b.at[done], sent.at[h - 1 + i]))
            copies[-1].start()
    for copy in copies:
        copy.wait()


def per_device(queries, keys, values, out_grad, norm_gain, log_decay, doc_ids):
    heads, rows, width = queries.shape
    seq = lax.axis_size("chip") * 2
    group = lax.axis_size("head")
    docs = doc_ids.reshape(1, rows)
    shape = lambda *dims: jax.ShapeDtypeStruct(dims, F32)
    block = shape(heads, rows, width)
    payload = shape(heads * width + EXTRA, width)
    product = 6 * heads * rows * width * width

    given = [keys, values, norm_gain, log_decay, docs]
    own, keys, values, norm_gain, log_decay, docs = kernel_call(
        state_body,
        (payload, *(jax.ShapeDtypeStruct(a.shape, a.dtype) for a in given)),
        product,
        "h" * len(given),
        scratch=(pltpu.SemaphoreType.DMA((len(given),)),),
    )(*(pltpu.with_memory_space_constraint(a, pltpu.HBM) for a in given))
    states = lax.all_gather(own, "core")
    chip_state = kernel_call(functools.partial(forward_join_body, heads), payload, product // 64)(states)
    ahead = [(i, i + 2 + 2 * (i % 2)) for i in range(seq)]
    moved = lax.ppermute(chip_state, ("chip", "core"), [(a, b) for a, b in ahead if b < seq])
    more = heads // 2 * rows
    asked, made, within, weighted = kernel_call(
        local_body,
        (
            shape(heads * rows + more + EXTRA, width),
            shape(2 * heads * rows - more, width),
            block,
            block,
        ),
        2 * product,
    )(queries, keys, values, out_grad, norm_gain, log_decay, docs, chip_state)
    asked = lax.all_gather(asked, "core")
    made, asked = lax.optimization_barrier((made, asked))
    made = lax.all_gather(made, "core")
    twice = shape(2, heads, rows, width)
    halves_twice = jax.ShapeDtypeStruct(twice.shape, BF16)
    high, low, start_high, start_low, passes = kernel_call(
        prepare_body, (halves_twice,) * 4 + (twice,), product // 4
    )(asked, states)
    moved, made, passes = lax.optimization_barrier((moved, made, passes))
    arrived = lax.all_gather(moved, "core")
    attended, sums = kernel_call(
        attended_body, (twice, shape(group, 2, 2 * rows)), 2 * product
    )(asked, made, states, high, low, passes, arrived)
    sums = lax.all_to_all(sums, "head", 0, 0, tiled=True)
    grad, chip_back, back = kernel_call(
        functools.partial(grad_state_body, heads * width * group),
        (twice, payload, shape(heads * width, width)),
        2 * product,
    )(sums, attended, asked, made, states, start_high, start_low)
    behind = [(i, i - 2 - 2 * (i % 2)) for i in range(seq)]
    moved_back = lax.ppermute(chip_back, ("chip", "core"), [(a, b) for a, b in behind if b >= 0])
    half = jax.ShapeDtypeStruct((heads, rows, width), BF16)
    query_grad, key_local, value_local, tails, *halves = kernel_call(
        main_grad_body, (block,) * 4 + (half,) * 4, 5 * product
    )(
        queries, keys, values, log_decay, docs, within, weighted, grad, states, arrived, chip_back
    )
    arrived_back = lax.all_gather(moved_back, "core")
    held = pltpu.VMEM((heads, rows, width), F32)
    key_grad, value_grad = kernel_call(
        last_grad_body,
        (block,) * 2,
        2 * product,
        "",
        "hh",
        (held, held, pltpu.SemaphoreType.DMA((heads,))),
    )(*halves, tails, docs, key_local, value_local, states, back, arrived_back)
    return query_grad, key_grad, value_grad


def solution(mesh):
    seq, head = mesh.devices.shape
    fine = Mesh(mesh.devices.reshape(seq // 2, 2, head), ("chip", "core", "head"))
    tokens = ("chip", "core")
    block = P("head", tokens, None)
    return jax.shard_map(
        per_device,
        mesh=fine,
        in_specs=(block, block, block, block, P("head", None), P("head", tokens), P(tokens)),
        out_specs=(block, block, block),
        check_vma=False,
    )
```

```python
import functools

import jax
import jax.numpy as jnp
from jax import lax
from jax.experimental import pallas as pl
from jax.experimental.pallas import tpu as pltpu
from jax.sharding import Mesh
from jax.sharding import PartitionSpec as P

EPSILON = 1e-06
F32 = jnp.float32
BF16 = jnp.bfloat16
NN = (((1,), (0,)), ((), ()))
NT = (((1,), (1,)), ((), ()))
TN = (((0,), (0,)), ((), ()))
VMEM_LIMIT = 12 * 2**20
LAST, FIRST, EXTRA = 4, 5, 8


def split(x):
    high = x.astype(BF16)
    return high, (x - high.astype(F32)).astype(BF16)


def dot3(left, right, dims):
    one = functools.partial(lax.dot_general, dimension_numbers=dims, preferred_element_type=F32)
    return one(left[0], right[0]) + (one(left[0], right[1]) + one(left[1], right[0]))


def kernel_call(body, outs, flops, kinds="", out_kinds="", scratch=(), aliases=()):
    spaces = {"h": pltpu.HBM, "s": pltpu.SMEM, "v": pltpu.VMEM}

    def call(*operands):
        of = [pl.BlockSpec(memory_space=spaces[c]) for c in kinds.ljust(len(operands), "v")]
        more = {}
        if out_kinds:
            made = [pl.BlockSpec(memory_space=spaces[c]) for c in out_kinds]
            more["out_specs"] = tuple(made)
        return pl.pallas_call(
            body,
            out_shape=outs,
            in_specs=of,
            scratch_shapes=list(scratch),
            input_output_aliases=dict(aliases),
            compiler_params=pltpu.CompilerParams(vmem_limit_bytes=VMEM_LIMIT),
            cost_estimate=pl.CostEstimate(flops=flops, bytes_accessed=2**20, transcendentals=0),
            **more,
        )(*operands)

    return call


def as_columns(row, rows):
    return jnp.broadcast_to(row, (rows, row.shape[1])).T


def lower_mask(rows):
    return lax.broadcasted_iota(jnp.int32, (rows, rows), 0) >= lax.broadcasted_iota(
        jnp.int32, (rows, rows), 1
    )


def running(lower, decay_row):
    return jnp.sum(jnp.where(lower, decay_row, 0.0), axis=1, keepdims=True)


def state_body(
    keys_hbm, values_hbm, gain_hbm, decay_hbm, docs_hbm,
    out, keys, values, gain, decay, docs, arrival,
):
    heads, rows, width = keys.shape
    pairs = [
        (docs_hbm, docs), (decay_hbm, decay), (keys_hbm, keys), (values_hbm, values), (gain_hbm, gain),
    ]
    copies = [pltpu.make_async_copy(a, b, arrival.at[i]) for i, (a, b) in enumerate(pairs)]
    for copy in copies:
        copy.start()
    lower = lower_mask(rows)
    base = heads * rows
    copies[0].wait()
    label_row = docs[...].astype(F32)
    label = as_columns(label_row, rows)[:, :1]
    last, first = label_row[:, rows - 1 :], label_row[:, :1]
    out[base + LAST : base + LAST + 1, :] = jnp.broadcast_to(last, (1, width))
    out[base + FIRST : base + FIRST + 1, :] = jnp.broadcast_to(first, (1, width))
    out[base + FIRST + 1 : base + EXTRA, :] = jnp.zeros((EXTRA - FIRST - 1, width), F32)
    copies[1].wait()
    weights = []
    for h in range(heads):
        cumulative = running(lower, decay[h : h + 1, :])
        total = cumulative[rows - 1 :, :]
        weights.append(jnp.where(label == last, jnp.exp(total - cumulative), 0.0))
        out[base + h : base + h + 1, :] = jnp.broadcast_to(total, (1, width))
    for copy in copies[2:]:
        copy.wait()
    for h in range(heads):
        state = dot3(split(keys[h] * weights[h]), split(values[h]), TN)
        out[h * width : (h + 1) * width, :] = state


def chip_meta(both, out, base, heads):
    width = out.shape[1]
    to = out.shape[0] - EXTRA
    out[to : to + heads, :] = both[0, base : base + heads, :] + both[1, base : base + heads, :]
    out[to + LAST : to + LAST + 1, :] = both[1, base + LAST : base + LAST + 1, :]
    out[to + FIRST : to + FIRST + 1, :] = both[0, base + FIRST : base + FIRST + 1, :]
    out[to + FIRST + 1 : to + EXTRA, :] = jnp.zeros((EXTRA - FIRST - 1, width), F32)


def row_of(ref, which, at):
    return ref[which, at : at + 1, :]


def forward_join_body(heads, both, out):
    width = out.shape[1]
    base = heads * width
    linked = row_of(both, 0, base + LAST) == row_of(both, 1, base + LAST)
    for h in range(heads):
        weight = jnp.where(linked, jnp.exp(row_of(both, 1, base + h)), 0.0)
        at = slice(h * width, (h + 1) * width)
        out[at, :] = both[1, at, :] + weight * both[0, at, :]
    chip_meta(both, out, base, heads)


def scaled_place(asked, made, h, heads, each, rows):
    half = heads // 2
    return (asked, each + h * rows) if h < half else (made, each + (h - half) * rows)


def token_rows(asked, made, h, heads, rows):
    at = slice(h * rows, (h + 1) * rows)
    of, row = scaled_place(asked, made, h, heads, heads * rows, rows)
    return asked[at, :], made[at, :], of[row : row + rows, :]


def local_body(
    queries, keys, values, out_grad, gain, decay, docs, sent, asked, made, within, weighted
):
    del sent
    heads, rows, width = queries.shape
    each = heads * rows
    lower = lower_mask(rows)
    label_row = docs[...].astype(F32)
    allowed = lower & (as_columns(label_row, rows) == label_row)
    for h in range(heads):
        cumulative = running(lower, decay[h : h + 1, :])
        spread = cumulative - jnp.broadcast_to(cumulative, (rows, rows)).T
        weight = jnp.where(allowed, jnp.exp(jnp.where(allowed, spread, 0.0)), 0.0)
        both = weight * dot3(split(queries[h]), split(keys[h]), NT)
        within[h] = weight
        weighted[h] = both
        at = h * rows
        asked[at : at + rows, :] = queries[h]
        made[at : at + rows, :] = dot3(split(both), split(values[h]), NN)
        of, row = scaled_place(asked, made, h, heads, each, rows)
        of[row : row + rows, :] = gain[h : h + 1, :] * out_grad[h]
    meta = asked.shape[0] - EXTRA
    asked[meta : meta + heads, :] = decay[...]
    asked[meta + heads : meta + EXTRA, :] = jnp.broadcast_to(label_row, (EXTRA - heads, rows))


def pick(condition, one, other):
    return jnp.where(condition, one, other)


def link(near_row, far_row, total_row):
    return jnp.where(near_row == far_row, jnp.exp(total_row), 0.0)


def states_ahead(states, arrived, h, width):
    base = arrived.shape[1] - EXTRA
    at = slice(h * width, (h + 1) * width)
    near = row_of(arrived, 0, base + LAST)
    inner = row_of(states, 0, base + LAST)
    far = link(near, row_of(arrived, 1, base + LAST), row_of(arrived, 0, base + h))
    outer_state = arrived[0, at, :] + far * arrived[1, at, :]
    passed = link(near, inner, row_of(states, 0, base + h))
    return outer_state, states[0, at, :] + passed * outer_state


def prepare_body(asked, states, high, low, start_high, start_low, passes):
    _, heads, rows, width = high.shape
    base = heads * width
    meta = asked.shape[1] - EXTRA
    lower = lower_mask(rows)
    for c in range(2):
        label = as_columns(row_of(asked, c, meta + heads), rows)
        started = label == row_of(states, c, base + FIRST)
        for h in range(heads):
            queries = asked[c, h * rows : (h + 1) * rows, :]
            high[c, h], low[c, h] = split(queries)
            decay = jnp.exp(running(lower, row_of(asked, c, meta + h)))
            passes[c, h] = jnp.broadcast_to(decay, (rows, width))
            start_high[c, h], start_low[c, h] = split((queries * jnp.where(started, decay, 0.0)).T)


def attended_body(
    asked, made, states, high, low, passes, arrived, attended, sums
):
    _, heads, rows, width = attended.shape
    base = heads * width
    meta = asked.shape[1] - EXTRA
    near = row_of(arrived, 0, base + LAST)
    inner = row_of(states, 0, base + LAST)
    allowed = [
        as_columns(row_of(asked, c, meta + heads), rows) == label
        for c, label in enumerate((near, inner))
    ]
    squares = [jnp.zeros((rows, width), F32)] * 2
    inners = [jnp.zeros((rows, width), F32)] * 2
    for h in range(heads):
        for c, state in enumerate(states_ahead(states, arrived, h, width)):
            _, local, scaled = token_rows(asked.at[c], made.at[c], h, heads, rows)
            reach = jnp.where(allowed[c], passes[c, h], 0.0)
            value = local + reach * dot3((high[c, h], low[c, h]), split(state), NN)
            attended[c, h] = value
            squares[c] += value * value
            inners[c] += scaled * value
    for c in range(2):
        two = jnp.concatenate(
            [
                jnp.sum(squares[c].T, axis=0, keepdims=True),
                jnp.sum(inners[c].T, axis=0, keepdims=True),
            ],
            axis=0,
        )
        for i in range(sums.shape[0]):
            sums[i, :, c * rows : (c + 1) * rows] = two


def grad_state_body(
    width_all, sums, attended, asked, made, states, start_high, start_low, grad, *outs_and_back
):
    *outs, back = outs_and_back
    _, heads, rows, width = attended.shape
    each = heads // len(outs)
    base = heads * width
    total = jnp.sum(sums[...], axis=0)
    inverse_row = lax.rsqrt(total[0:1, :] / width_all + EPSILON)
    coupling_row = total[1:2, :] / width_all * inverse_row * inverse_row
    first_label = row_of(states, 0, base + FIRST)
    second_label = row_of(states, 1, base + FIRST)
    inverse = [as_columns(inverse_row[:, c * rows : (c + 1) * rows], rows) for c in range(2)]
    coupling = [as_columns(coupling_row[:, c * rows : (c + 1) * rows], rows) for c in range(2)]
    for h in range(heads):
        at = slice(h * width, (h + 1) * width)
        of_cores = []
        for c in range(2):
            _, _, scaled = token_rows(asked.at[c], made.at[c], h, heads, rows)
            value = inverse[c] * (scaled - attended[c, h] * coupling[c])
            grad[c, h] = value
            of_cores.append(dot3((start_high[c, h], start_low[c, h]), split(value), NN))
        back[at, :] = of_cores[1]
        passed = link(first_label, second_label, row_of(states, 0, base + h))
        to = h % each * width
        outs[h // each][to : to + width, :] = of_cores[0] + passed * of_cores[1]
    for out in outs:
        chip_meta(states, out, base, heads)


def main_grad_body(
    queries, keys, values, decay, docs, within, weighted, grad, states, arrived, sent, sent_later,
    query_grad, key_local, value_local, tails, *halves,
):
    del sent, sent_later
    rows, width = queries.shape[1:]
    base = arrived.shape[1] - EXTRA
    lower = lower_mask(rows)
    second = lax.axis_index("core") == 1
    near = pick(second, row_of(states, 0, base + LAST), row_of(arrived, 0, base + LAST))
    ahead = as_columns(docs[...].astype(F32), rows) == near
    for h in range(queries.shape[0]):
        of_grad = split(grad[lax.axis_index("core"), h])
        of_keys = split(keys[h])
        of_values = split(values[h])
        of_both = split(within[h] * dot3(of_grad, of_values, NT))
        cumulative = running(lower, decay[h : h + 1, :])
        outer_state, inner_state = states_ahead(states, arrived, h, width)
        of_state = split(pick(second, inner_state, outer_state))
        reach = jnp.where(ahead, jnp.exp(cumulative), 0.0)
        query_grad[h] = dot3(of_both, of_keys, NN) + reach * dot3(of_grad, of_state, NT)
        key_local[h] = dot3(of_both, split(queries[h]), TN)
        value_local[h] = dot3(split(weighted[h]), of_grad, TN)
        for half, part in zip(halves, (*of_keys, *of_values)):
            half[h] = part
        tail = jnp.exp(cumulative[rows - 1 :, :] - cumulative)
        tails[h] = jnp.broadcast_to(tail, tails.shape[1:])


def last_grad_body(
    start, keys_high, keys_low, values_high, values_low, tails, docs, key_local, value_local,
    meta, back, arrived, *rest,
):
    key_grad_hbm, value_grad_hbm, key_grad, value_grad, sent = rest[-5:]
    heads, rows, width = tails.shape
    base = heads * width
    end = arrived.shape[1] - EXTRA
    first = lax.axis_index("core") == 0
    near = row_of(arrived, 0, end + FIRST)
    chained = near == row_of(arrived, 1, end + FIRST)
    inner = row_of(meta, 1, base + FIRST)
    linked = inner == near
    ahead = as_columns(docs[...].astype(F32), rows) == jnp.where(first, inner, near)
    for i in range(end // width):
        h = start + i
        at = slice(i * width, (i + 1) * width)
        weight = jnp.where(chained, jnp.exp(row_of(arrived, 0, end + h)), 0.0)
        state = arrived[0, at, :] + weight * arrived[1, at, :]
        passed = jnp.where(linked, jnp.exp(row_of(meta, 1, base + h)), 0.0)
        nearer = back[h * width : (h + 1) * width, :] + passed * state
        of_state = split(jnp.where(first, nearer, state))
        to_next = jnp.where(ahead, tails[h], 0.0)
        key_grad[i] = key_local[h] + to_next * dot3((values_high[h], values_low[h]), of_state, NT)
        value_grad[i] = value_local[h] + to_next * dot3((keys_high[h], keys_low[h]), of_state, NN)
    done = slice(start, start + end // width)
    copies = [
        pltpu.make_async_copy(key_grad, key_grad_hbm.at[done], sent.at[0]),
        pltpu.make_async_copy(value_grad, value_grad_hbm.at[done], sent.at[1]),
    ]
    for copy in copies:
        copy.start()
    for copy in copies:
        copy.wait()


def per_device(queries, keys, values, out_grad, norm_gain, log_decay, doc_ids):
    heads, rows, width = queries.shape
    seq = lax.axis_size("chip") * 2
    group = lax.axis_size("head")
    docs = doc_ids.reshape(1, rows)
    shape = lambda *dims: jax.ShapeDtypeStruct(dims, F32)
    block = shape(heads, rows, width)
    payload = shape(heads * width + EXTRA, width)
    product = 6 * heads * rows * width * width

    given = [keys, values, norm_gain, log_decay, docs]
    own, keys, values, norm_gain, log_decay, docs = kernel_call(
        state_body,
        (payload, *(jax.ShapeDtypeStruct(a.shape, a.dtype) for a in given)),
        product,
        "h" * len(given),
        scratch=(pltpu.SemaphoreType.DMA((len(given),)),),
    )(*(pltpu.with_memory_space_constraint(a, pltpu.HBM) for a in given))
    states = lax.all_gather(own, "core")
    chip_state = kernel_call(functools.partial(forward_join_body, heads), payload, product // 64)(states)
    ahead = [(i, i + 2 + 2 * (i % 2)) for i in range(seq)]
    moved = lax.ppermute(chip_state, ("chip", "core"), [(a, b) for a, b in ahead if b < seq])
    more = heads // 2 * rows
    asked, made, within, weighted = kernel_call(
        local_body,
        (
            shape(heads * rows + more + EXTRA, width),
            shape(2 * heads * rows - more, width),
            block,
            block,
        ),
        2 * product,
    )(queries, keys, values, out_grad, norm_gain, log_decay, docs, chip_state)
    asked = lax.all_gather(asked, "core")
    made, asked = lax.optimization_barrier((made, asked))
    made = lax.all_gather(made, "core")
    twice = shape(2, heads, rows, width)
    halves_twice = jax.ShapeDtypeStruct(twice.shape, BF16)
    high, low, start_high, start_low, passes = kernel_call(
        prepare_body, (halves_twice,) * 4 + (twice,), product // 4
    )(asked, states)
    moved, made, passes = lax.optimization_barrier((moved, made, passes))
    arrived = lax.all_gather(moved, "core")
    attended, sums = kernel_call(
        attended_body, (twice, shape(group, 2, 2 * rows)), 2 * product
    )(asked, made, states, high, low, passes, arrived)
    sums = lax.all_to_all(sums, "head", 0, 0, tiled=True)
    part = shape(heads // 2 * width + EXTRA, width)
    grad, *chip_backs, back = kernel_call(
        functools.partial(grad_state_body, heads * width * group),
        (twice, part, part, shape(heads * width, width)),
        2 * product,
    )(sums, attended, asked, made, states, start_high, start_low)
    behind = [(i, i - 2 - 2 * (i % 2)) for i in range(seq)]
    to = [(a, b) for a, b in behind if b >= 0]
    moved_backs = [lax.ppermute(a, ("chip", "core"), to) for a in chip_backs]
    half = jax.ShapeDtypeStruct((heads, rows, width), BF16)
    query_grad, key_local, value_local, tails, *halves = kernel_call(
        main_grad_body, (block,) * 4 + (half,) * 4, 5 * product
    )(
        queries, keys, values, log_decay, docs, within, weighted, grad, states, arrived, *chip_backs
    )
    held = pltpu.VMEM((heads // 2, rows, width), F32)
    local = (*halves, tails, docs, key_local, value_local, states, back)
    grads = ()
    for i, moved_back in enumerate(moved_backs):
        if i:
            moved_back, *grads = lax.optimization_barrier((moved_back, *grads))
        arrived_back = lax.all_gather(moved_back, "core")
        operands = (*local, arrived_back, *grads)
        grads = kernel_call(
            functools.partial(last_grad_body, i * (heads // 2)),
            (block,) * 2,
            product,
            "v" * (len(local) + 1) + "h" * len(grads),
            "hh",
            (held, held, pltpu.SemaphoreType.DMA((2,))),
            [(len(local) + 1 + n, n) for n in range(len(grads))],
        )(*operands)
    key_grad, value_grad = grads
    return query_grad, key_grad, value_grad


def solution(mesh):
    seq, head = mesh.devices.shape
    fine = Mesh(mesh.devices.reshape(seq // 2, 2, head), ("chip", "core", "head"))
    tokens = ("chip", "core")
    block = P("head", tokens, None)
    return jax.shard_map(
        per_device,
        mesh=fine,
        in_specs=(block, block, block, block, P("head", None), P("head", tokens), P(tokens)),
        out_specs=(block, block, block),
        check_vma=False,
    )
```

```python
import functools

import jax
import jax.numpy as jnp
from jax import lax
from jax.experimental import pallas as pl
from jax.experimental.pallas import tpu as pltpu
from jax.sharding import Mesh
from jax.sharding import PartitionSpec as P

EPSILON = 1e-06
F32 = jnp.float32
BF16 = jnp.bfloat16
NN = (((1,), (0,)), ((), ()))
NT = (((1,), (1,)), ((), ()))
TN = (((0,), (0,)), ((), ()))
VMEM_LIMIT = 12 * 2**20
LAST, FIRST, EXTRA = 4, 5, 8


def split(x):
    high = x.astype(BF16)
    return high, (x - high.astype(F32)).astype(BF16)


def dot3(left, right, dims):
    one = functools.partial(lax.dot_general, dimension_numbers=dims, preferred_element_type=F32)
    return one(left[0], right[0]) + (one(left[0], right[1]) + one(left[1], right[0]))


def kernel_call(body, outs, flops, kinds="", out_kinds="", scratch=()):
    spaces = {"h": pltpu.HBM, "s": pltpu.SMEM, "v": pltpu.VMEM}

    def call(*operands):
        of = [pl.BlockSpec(memory_space=spaces[c]) for c in kinds.ljust(len(operands), "v")]
        more = {}
        if out_kinds:
            made = [pl.BlockSpec(memory_space=spaces[c]) for c in out_kinds]
            more["out_specs"] = tuple(made)
        return pl.pallas_call(
            body,
            out_shape=outs,
            in_specs=of,
            scratch_shapes=list(scratch),
            compiler_params=pltpu.CompilerParams(vmem_limit_bytes=VMEM_LIMIT),
            cost_estimate=pl.CostEstimate(flops=flops, bytes_accessed=2**20, transcendentals=0),
            **more,
        )(*operands)

    return call


def as_columns(row, rows):
    return jnp.broadcast_to(row, (rows, row.shape[1])).T


def lower_mask(rows):
    return lax.broadcasted_iota(jnp.int32, (rows, rows), 0) >= lax.broadcasted_iota(
        jnp.int32, (rows, rows), 1
    )


def running(lower, decay_row):
    return jnp.sum(jnp.where(lower, decay_row, 0.0), axis=1, keepdims=True)


def state_body(
    keys_hbm, values_hbm, gain_hbm, decay_hbm, docs_hbm,
    out, keys, values, gain, decay, docs, arrival,
):
    heads, rows, width = keys.shape
    pairs = [
        (docs_hbm, docs), (decay_hbm, decay), (keys_hbm, keys), (values_hbm, values), (gain_hbm, gain),
    ]
    copies = [pltpu.make_async_copy(a, b, arrival.at[i]) for i, (a, b) in enumerate(pairs)]
    for copy in copies:
        copy.start()
    lower = lower_mask(rows)
    base = heads * rows
    copies[0].wait()
    label_row = docs[...].astype(F32)
    label = as_columns(label_row, rows)[:, :1]
    last, first = label_row[:, rows - 1 :], label_row[:, :1]
    out[base + LAST : base + LAST + 1, :] = jnp.broadcast_to(last, (1, width))
    out[base + FIRST : base + FIRST + 1, :] = jnp.broadcast_to(first, (1, width))
    out[base + FIRST + 1 : base + EXTRA, :] = jnp.zeros((EXTRA - FIRST - 1, width), F32)
    copies[1].wait()
    weights = []
    for h in range(heads):
        cumulative = running(lower, decay[h : h + 1, :])
        total = cumulative[rows - 1 :, :]
        weights.append(jnp.where(label == last, jnp.exp(total - cumulative), 0.0))
        out[base + h : base + h + 1, :] = jnp.broadcast_to(total, (1, width))
    for copy in copies[2:]:
        copy.wait()
    for h in range(heads):
        state = dot3(split(keys[h]), split(values[h] * weights[h]), TN)
        out[h * width : (h + 1) * width, :] = state


def chip_meta(both, out, base, heads):
    width = out.shape[1]
    out[base : base + heads, :] = both[0, base : base + heads, :] + both[1, base : base + heads, :]
    out[base + LAST : base + LAST + 1, :] = both[1, base + LAST : base + LAST + 1, :]
    out[base + FIRST : base + FIRST + 1, :] = both[0, base + FIRST : base + FIRST + 1, :]
    out[base + FIRST + 1 : base + EXTRA, :] = jnp.zeros((EXTRA - FIRST - 1, width), F32)


def row_of(ref, which, at):
    return ref[which, at : at + 1, :]


def forward_join_body(heads, both, out):
    width = out.shape[1]
    base = heads * width
    linked = row_of(both, 0, base + LAST) == row_of(both, 1, base + LAST)
    for h in range(heads):
        weight = jnp.where(linked, jnp.exp(row_of(both, 1, base + h)), 0.0)
        at = slice(h * width, (h + 1) * width)
        out[at, :] = both[1, at, :] + weight * both[0, at, :]
    chip_meta(both, out, base, heads)


def scaled_place(asked, made, h, heads, each, rows):
    half = heads // 2
    return (asked, each + h * rows) if h < half else (made, each + (h - half) * rows)


def token_rows(asked, made, h, heads, rows):
    at = slice(h * rows, (h + 1) * rows)
    of, row = scaled_place(asked, made, h, heads, heads * rows, rows)
    return asked[at, :], made[at, :], of[row : row + rows, :]


def local_body(
    queries, keys, values, out_grad, gain, decay, docs, sent, asked, made, within, weighted
):
    del sent
    heads, rows, width = queries.shape
    each = heads * rows
    lower = lower_mask(rows)
    label_row = docs[...].astype(F32)
    allowed = lower & (as_columns(label_row, rows) == label_row)
    for h in range(heads):
        cumulative = running(lower, decay[h : h + 1, :])
        spread = cumulative - jnp.broadcast_to(cumulative, (rows, rows)).T
        weight = jnp.where(allowed, jnp.exp(jnp.where(allowed, spread, 0.0)), 0.0)
        both = weight * dot3(split(queries[h]), split(keys[h]), NT)
        within[h] = weight
        weighted[h] = both
        at = h * rows
        asked[at : at + rows, :] = queries[h]
        made[at : at + rows, :] = dot3(split(both), split(values[h]), NN)
        of, row = scaled_place(asked, made, h, heads, each, rows)
        of[row : row + rows, :] = gain[h : h + 1, :] * out_grad[h]
    meta = asked.shape[0] - EXTRA
    asked[meta : meta + heads, :] = decay[...]
    asked[meta + heads : meta + EXTRA, :] = jnp.broadcast_to(label_row, (EXTRA - heads, rows))


def pick(condition, one, other):
    return jnp.where(condition, one, other)


def link(near_row, far_row, total_row):
    return jnp.where(near_row == far_row, jnp.exp(total_row), 0.0)


def states_ahead(states, arrived, h, width):
    base = arrived.shape[1] - EXTRA
    at = slice(h * width, (h + 1) * width)
    near = row_of(arrived, 0, base + LAST)
    inner = row_of(states, 0, base + LAST)
    far = link(near, row_of(arrived, 1, base + LAST), row_of(arrived, 0, base + h))
    outer_state = arrived[0, at, :] + far * arrived[1, at, :]
    passed = link(near, inner, row_of(states, 0, base + h))
    return outer_state, states[0, at, :] + passed * outer_state


def prepare_body(asked, states, high, low, start_high, start_low, passes):
    _, heads, rows, width = high.shape
    base = heads * width
    meta = asked.shape[1] - EXTRA
    lower = lower_mask(rows)
    for c in range(2):
        label = as_columns(row_of(asked, c, meta + heads), rows)
        started = label == row_of(states, c, base + FIRST)
        for h in range(heads):
            queries = asked[c, h * rows : (h + 1) * rows, :]
            high[c, h], low[c, h] = split(queries)
            decay = jnp.exp(running(lower, row_of(asked, c, meta + h)))
            passes[c, h] = jnp.broadcast_to(decay, (rows, width))
            start_high[c, h], start_low[c, h] = split((queries * jnp.where(started, decay, 0.0)).T)


def attended_body(
    asked, made, states, high, low, passes, arrived, attended, sums
):
    _, heads, rows, width = attended.shape
    base = heads * width
    meta = asked.shape[1] - EXTRA
    near = row_of(arrived, 0, base + LAST)
    inner = row_of(states, 0, base + LAST)
    allowed = [
        as_columns(row_of(asked, c, meta + heads), rows) == label
        for c, label in enumerate((near, inner))
    ]
    squares = [jnp.zeros((rows, width), F32)] * 2
    inners = [jnp.zeros((rows, width), F32)] * 2
    for h in range(heads):
        for c, state in enumerate(states_ahead(states, arrived, h, width)):
            _, local, scaled = token_rows(asked.at[c], made.at[c], h, heads, rows)
            reach = jnp.where(allowed[c], passes[c, h], 0.0)
            value = local + reach * dot3((high[c, h], low[c, h]), split(state), NN)
            attended[c, h] = value
            squares[c] += value * value
            inners[c] += scaled * value
    for c in range(2):
        two = jnp.concatenate(
            [
                jnp.sum(squares[c].T, axis=0, keepdims=True),
                jnp.sum(inners[c].T, axis=0, keepdims=True),
            ],
            axis=0,
        )
        for i in range(sums.shape[0]):
            sums[i, :, c * rows : (c + 1) * rows] = two


def grad_state_body(
    width_all, sums, attended, asked, made, states, start_high, start_low, grad, out, back
):
    _, heads, rows, width = attended.shape
    base = heads * width
    second = lax.axis_index("core") == 1
    total = jnp.sum(sums[...], axis=0)
    inverse_row = lax.rsqrt(total[0:1, :] / width_all + EPSILON)
    coupling_row = total[1:2, :] / width_all * inverse_row * inverse_row
    first_label = row_of(states, 0, base + FIRST)
    second_label = row_of(states, 1, base + FIRST)
    inverse = [as_columns(inverse_row[:, c * rows : (c + 1) * rows], rows) for c in range(2)]
    coupling = [as_columns(coupling_row[:, c * rows : (c + 1) * rows], rows) for c in range(2)]
    for h in range(heads):
        at = slice(h * width, (h + 1) * width)
        of_cores, of_both = [], []
        for c in range(2):
            _, _, scaled = token_rows(asked.at[c], made.at[c], h, heads, rows)
            value = inverse[c] * (scaled - attended[c, h] * coupling[c])
            of_both.append(value)
            of_cores.append(dot3((start_high[c, h], start_low[c, h]), split(value), NN))
        grad[h] = pick(second, of_both[1], of_both[0])
        back[at, :] = of_cores[1]
        passed = link(first_label, second_label, row_of(states, 0, base + h))
        out[at, :] = of_cores[0] + passed * of_cores[1]
    chip_meta(states, out, base, heads)


def main_grad_body(
    queries, keys, values, decay, docs, within, weighted, grad, states, arrived, sent,
    query_grad, key_local, value_local, tails, *halves,
):
    del sent
    rows, width = queries.shape[1:]
    base = arrived.shape[1] - EXTRA
    lower = lower_mask(rows)
    second = lax.axis_index("core") == 1
    near = pick(second, row_of(states, 0, base + LAST), row_of(arrived, 0, base + LAST))
    ahead = as_columns(docs[...].astype(F32), rows) == near
    for h in range(queries.shape[0]):
        of_grad = split(grad[h])
        of_keys = split(keys[h])
        of_values = split(values[h])
        of_both = split(within[h] * dot3(of_grad, of_values, NT))
        cumulative = running(lower, decay[h : h + 1, :])
        outer_state, inner_state = states_ahead(states, arrived, h, width)
        of_state = split(pick(second, inner_state, outer_state))
        reach = jnp.where(ahead, jnp.exp(cumulative), 0.0)
        query_grad[h] = dot3(of_both, of_keys, NN) + reach * dot3(of_grad, of_state, NT)
        key_local[h] = dot3(of_both, split(queries[h]), TN)
        value_local[h] = dot3(split(weighted[h]), of_grad, TN)
        for half, part in zip(halves, (*of_keys, *of_values)):
            half[h] = part
        tail = jnp.exp(cumulative[rows - 1 :, :] - cumulative)
        tails[h] = jnp.broadcast_to(tail, tails.shape[1:])


def last_grad_body(
    keys_high, keys_low, values_high, values_low, tails, docs, key_local, value_local,
    meta, back, arrived, key_grad_hbm, value_grad_hbm, key_grad, value_grad, sent,
):
    heads, rows, width = tails.shape
    base = heads * width
    first = lax.axis_index("core") == 0
    near = row_of(arrived, 0, base + FIRST)
    chained = near == row_of(arrived, 1, base + FIRST)
    inner = row_of(meta, 1, base + FIRST)
    linked = inner == near
    ahead = as_columns(docs[...].astype(F32), rows) == jnp.where(first, inner, near)
    copies = []
    for h in range(heads):
        at = slice(h * width, (h + 1) * width)
        weight = jnp.where(chained, jnp.exp(row_of(arrived, 0, base + h)), 0.0)
        state = arrived[0, at, :] + weight * arrived[1, at, :]
        passed = jnp.where(linked, jnp.exp(row_of(meta, 1, base + h)), 0.0)
        of_state = split(jnp.where(first, back[at, :] + passed * state, state))
        to_next = jnp.where(ahead, tails[h], 0.0)
        key_grad[h] = key_local[h] + to_next * dot3((values_high[h], values_low[h]), of_state, NT)
        value_grad[h] = value_local[h] + to_next * dot3((keys_high[h], keys_low[h]), of_state, NN)
        if h % 2 == 0:
            continue
        for i, (a, b) in enumerate(((key_grad, key_grad_hbm), (value_grad, value_grad_hbm))):
            done = slice(h - 1, h + 1)
            copies.append(pltpu.make_async_copy(a.at[done], b.at[done], sent.at[h - 1 + i]))
            copies[-1].start()
    for copy in copies:
        copy.wait()


def per_device(queries, keys, values, out_grad, norm_gain, log_decay, doc_ids):
    heads, rows, width = queries.shape
    seq = lax.axis_size("chip") * 2
    group = lax.axis_size("head")
    docs = doc_ids.reshape(1, rows)
    shape = lambda *dims: jax.ShapeDtypeStruct(dims, F32)
    block = shape(heads, rows, width)
    payload = shape(heads * width + EXTRA, width)
    product = 6 * heads * rows * width * width

    given = [keys, values, norm_gain, log_decay, docs]
    own, keys, values, norm_gain, log_decay, docs = kernel_call(
        state_body,
        (payload, *(jax.ShapeDtypeStruct(a.shape, a.dtype) for a in given)),
        product,
        "h" * len(given),
        scratch=(pltpu.SemaphoreType.DMA((len(given),)),),
    )(*(pltpu.with_memory_space_constraint(a, pltpu.HBM) for a in given))
    states = lax.all_gather(own, "core")
    chip_state = kernel_call(functools.partial(forward_join_body, heads), payload, product // 64)(states)
    ahead = [(i, i + 2 + 2 * (i % 2)) for i in range(seq)]
    moved = lax.ppermute(chip_state, ("chip", "core"), [(a, b) for a, b in ahead if b < seq])
    more = heads // 2 * rows
    asked, made, within, weighted = kernel_call(
        local_body,
        (
            shape(heads * rows + more + EXTRA, width),
            shape(2 * heads * rows - more, width),
            block,
            block,
        ),
        2 * product,
    )(queries, keys, values, out_grad, norm_gain, log_decay, docs, chip_state)
    asked = lax.all_gather(asked, "core")
    made, asked = lax.optimization_barrier((made, asked))
    made = lax.all_gather(made, "core")
    twice = shape(2, heads, rows, width)
    halves_twice = jax.ShapeDtypeStruct(twice.shape, BF16)
    high, low, start_high, start_low, passes = kernel_call(
        prepare_body, (halves_twice,) * 4 + (twice,), product // 4
    )(asked, states)
    moved, made, passes = lax.optimization_barrier((moved, made, passes))
    arrived = lax.all_gather(moved, "core")
    attended, sums = kernel_call(
        attended_body, (twice, shape(group, 2, 2 * rows)), 2 * product
    )(asked, made, states, high, low, passes, arrived)
    sums = lax.all_to_all(sums, "head", 0, 0, tiled=True)
    grad, chip_back, back = kernel_call(
        functools.partial(grad_state_body, heads * width * group),
        (block, payload, shape(heads * width, width)),
        2 * product,
    )(sums, attended, asked, made, states, start_high, start_low)
    behind = [(i, i - 2 - 2 * (i % 2)) for i in range(seq)]
    moved_back = lax.ppermute(chip_back, ("chip", "core"), [(a, b) for a, b in behind if b >= 0])
    half = jax.ShapeDtypeStruct((heads, rows, width), BF16)
    query_grad, key_local, value_local, tails, *halves = kernel_call(
        main_grad_body, (block,) * 4 + (half,) * 4, 5 * product
    )(
        queries, keys, values, log_decay, docs, within, weighted, grad, states, arrived, chip_back
    )
    arrived_back = lax.all_gather(moved_back, "core")
    held = pltpu.VMEM((heads, rows, width), F32)
    key_grad, value_grad = kernel_call(
        last_grad_body,
        (block,) * 2,
        2 * product,
        "",
        "hh",
        (held, held, pltpu.SemaphoreType.DMA((heads,))),
    )(*halves, tails, docs, key_local, value_local, states, back, arrived_back)
    return query_grad, key_grad, value_grad


def solution(mesh):
    seq, head = mesh.devices.shape
    fine = Mesh(mesh.devices.reshape(seq // 2, 2, head), ("chip", "core", "head"))
    tokens = ("chip", "core")
    block = P("head", tokens, None)
    return jax.shard_map(
        per_device,
        mesh=fine,
        in_specs=(block, block, block, block, P("head", None), P("head", tokens), P(tokens)),
        out_specs=(block, block, block),
        check_vma=False,
    )
```

```python
import functools

import jax
import jax.numpy as jnp
from jax import lax
from jax.experimental import pallas as pl
from jax.experimental.pallas import tpu as pltpu
from jax.sharding import Mesh
from jax.sharding import PartitionSpec as P

EPSILON = 1e-06
F32 = jnp.float32
BF16 = jnp.bfloat16
NN = (((1,), (0,)), ((), ()))
NT = (((1,), (1,)), ((), ()))
TN = (((0,), (0,)), ((), ()))
VMEM_LIMIT = 12 * 2**20
LAST, FIRST, EXTRA = 4, 5, 8


def split(x):
    high = x.astype(BF16)
    return high, (x - high.astype(F32)).astype(BF16)


def dot3(left, right, dims):
    one = functools.partial(lax.dot_general, dimension_numbers=dims, preferred_element_type=F32)
    return one(left[0], right[0]) + (one(left[0], right[1]) + one(left[1], right[0]))


def kernel_call(body, outs, flops, kinds="", out_kinds="", scratch=()):
    spaces = {"h": pltpu.HBM, "s": pltpu.SMEM, "v": pltpu.VMEM}

    def call(*operands):
        of = [pl.BlockSpec(memory_space=spaces[c]) for c in kinds.ljust(len(operands), "v")]
        more = {}
        if out_kinds:
            made = [pl.BlockSpec(memory_space=spaces[c]) for c in out_kinds]
            more["out_specs"] = tuple(made)
        return pl.pallas_call(
            body,
            out_shape=outs,
            in_specs=of,
            scratch_shapes=list(scratch),
            compiler_params=pltpu.CompilerParams(vmem_limit_bytes=VMEM_LIMIT),
            cost_estimate=pl.CostEstimate(flops=flops, bytes_accessed=2**20, transcendentals=0),
            **more,
        )(*operands)

    return call


def as_columns(row, rows):
    return jnp.broadcast_to(row, (rows, row.shape[1])).T


def lower_mask(rows):
    return lax.broadcasted_iota(jnp.int32, (rows, rows), 0) >= lax.broadcasted_iota(
        jnp.int32, (rows, rows), 1
    )


def running(lower, decay_row):
    return jnp.sum(jnp.where(lower, decay_row, 0.0), axis=1, keepdims=True)


def state_body(
    keys_hbm, values_hbm, gain_hbm, decay_hbm, docs_hbm,
    out, keys, values, gain, decay, docs, arrival,
):
    heads, rows, width = keys.shape
    pairs = [
        (docs_hbm, docs), (decay_hbm, decay), (keys_hbm, keys), (values_hbm, values), (gain_hbm, gain),
    ]
    copies = [pltpu.make_async_copy(a, b, arrival.at[i]) for i, (a, b) in enumerate(pairs)]
    for copy in copies:
        copy.start()
    lower = lower_mask(rows)
    base = heads * rows
    copies[0].wait()
    label_row = docs[...].astype(F32)
    label = as_columns(label_row, rows)[:, :1]
    last, first = label_row[:, rows - 1 :], label_row[:, :1]
    out[base + LAST : base + LAST + 1, :] = jnp.broadcast_to(last, (1, width))
    out[base + FIRST : base + FIRST + 1, :] = jnp.broadcast_to(first, (1, width))
    out[base + FIRST + 1 : base + EXTRA, :] = jnp.zeros((EXTRA - FIRST - 1, width), F32)
    copies[1].wait()
    weights = []
    for h in range(heads):
        cumulative = running(lower, decay[h : h + 1, :])
        total = cumulative[rows - 1 :, :]
        weights.append(jnp.where(label == last, jnp.exp(total - cumulative), 0.0))
        out[base + h : base + h + 1, :] = jnp.broadcast_to(total, (1, width))
    for copy in copies[2:]:
        copy.wait()
    for h in range(heads):
        state = dot3(split(keys[h]), split(values[h] * weights[h]), TN)
        out[h * width : (h + 1) * width, :] = state


def chip_meta(both, out, base, heads):
    width = out.shape[1]
    out[base : base + heads, :] = both[0, base : base + heads, :] + both[1, base : base + heads, :]
    out[base + LAST : base + LAST + 1, :] = both[1, base + LAST : base + LAST + 1, :]
    out[base + FIRST : base + FIRST + 1, :] = both[0, base + FIRST : base + FIRST + 1, :]
    out[base + FIRST + 1 : base + EXTRA, :] = jnp.zeros((EXTRA - FIRST - 1, width), F32)


def row_of(ref, which, at):
    return ref[which, at : at + 1, :]


def forward_join_body(heads, both, out):
    width = out.shape[1]
    base = heads * width
    linked = row_of(both, 0, base + LAST) == row_of(both, 1, base + LAST)
    for h in range(heads):
        weight = jnp.where(linked, jnp.exp(row_of(both, 1, base + h)), 0.0)
        at = slice(h * width, (h + 1) * width)
        out[at, :] = both[1, at, :] + weight * both[0, at, :]
    chip_meta(both, out, base, heads)


def scaled_place(asked, made, h, heads, each, rows):
    half = heads // 2
    return (asked, each + h * rows) if h < half else (made, each + (h - half) * rows)


def token_rows(asked, made, h, heads, rows):
    at = slice(h * rows, (h + 1) * rows)
    of, row = scaled_place(asked, made, h, heads, heads * rows, rows)
    return asked[at, :], made[at, :], of[row : row + rows, :]


def local_body(
    queries, keys, values, out_grad, gain, decay, docs, sent, asked, made, within, weighted
):
    del sent
    heads, rows, width = queries.shape
    each = heads * rows
    lower = lower_mask(rows)
    label_row = docs[...].astype(F32)
    allowed = lower & (as_columns(label_row, rows) == label_row)
    for h in range(heads):
        cumulative = running(lower, decay[h : h + 1, :])
        spread = cumulative - jnp.broadcast_to(cumulative, (rows, rows)).T
        weight = jnp.where(allowed, jnp.exp(jnp.where(allowed, spread, 0.0)), 0.0)
        both = weight * dot3(split(queries[h]), split(keys[h]), NT)
        within[h] = weight
        weighted[h] = both
        at = h * rows
        asked[at : at + rows, :] = queries[h]
        made[at : at + rows, :] = dot3(split(both), split(values[h]), NN)
        of, row = scaled_place(asked, made, h, heads, each, rows)
        of[row : row + rows, :] = gain[h : h + 1, :] * out_grad[h]
    meta = asked.shape[0] - EXTRA
    asked[meta : meta + heads, :] = decay[...]
    asked[meta + heads : meta + EXTRA, :] = jnp.broadcast_to(label_row, (EXTRA - heads, rows))


def pick(condition, one, other):
    return jnp.where(condition, one, other)


def link(near_row, far_row, total_row):
    return jnp.where(near_row == far_row, jnp.exp(total_row), 0.0)


def states_ahead(states, arrived, h, width):
    base = arrived.shape[1] - EXTRA
    at = slice(h * width, (h + 1) * width)
    near = row_of(arrived, 0, base + LAST)
    inner = row_of(states, 0, base + LAST)
    far = link(near, row_of(arrived, 1, base + LAST), row_of(arrived, 0, base + h))
    outer_state = arrived[0, at, :] + far * arrived[1, at, :]
    passed = link(near, inner, row_of(states, 0, base + h))
    return outer_state, states[0, at, :] + passed * outer_state


def prepare_body(asked, states, high, low, start_high, start_low, passes):
    _, heads, rows, width = high.shape
    base = heads * width
    meta = asked.shape[1] - EXTRA
    lower = lower_mask(rows)
    for c in range(2):
        label = as_columns(row_of(asked, c, meta + heads), rows)
        started = label == row_of(states, c, base + FIRST)
        for h in range(heads):
            queries = asked[c, h * rows : (h + 1) * rows, :]
            high[c, h], low[c, h] = split(queries)
            decay = jnp.exp(running(lower, row_of(asked, c, meta + h)))
            passes[c, h] = jnp.broadcast_to(decay, (rows, width))
            start_high[c, h], start_low[c, h] = split((queries * jnp.where(started, decay, 0.0)).T)


def attended_body(
    asked, made, states, high, low, passes, arrived, attended, sums
):
    _, heads, rows, width = attended.shape
    base = heads * width
    meta = asked.shape[1] - EXTRA
    near = row_of(arrived, 0, base + LAST)
    inner = row_of(states, 0, base + LAST)
    allowed = [
        as_columns(row_of(asked, c, meta + heads), rows) == label
        for c, label in enumerate((near, inner))
    ]
    squares = [jnp.zeros((rows, width), F32)] * 2
    inners = [jnp.zeros((rows, width), F32)] * 2
    for h in range(heads):
        for c, state in enumerate(states_ahead(states, arrived, h, width)):
            _, local, scaled = token_rows(asked.at[c], made.at[c], h, heads, rows)
            reach = jnp.where(allowed[c], passes[c, h], 0.0)
            value = local + reach * dot3((high[c, h], low[c, h]), split(state), NN)
            attended[c, h] = value
            squares[c] += value * value
            inners[c] += scaled * value
    for c in range(2):
        two = jnp.concatenate(
            [
                jnp.sum(squares[c].T, axis=0, keepdims=True),
                jnp.sum(inners[c].T, axis=0, keepdims=True),
            ],
            axis=0,
        )
        for i in range(sums.shape[0]):
            sums[i, :, c * rows : (c + 1) * rows] = two


def grad_state_body(
    width_all, sums, attended, asked, made, states, start_high, start_low, grad, out, back
):
    _, heads, rows, width = attended.shape
    base = heads * width
    second = lax.axis_index("core") == 1
    total = jnp.sum(sums[...], axis=0)
    inverse_row = lax.rsqrt(total[0:1, :] / width_all + EPSILON)
    coupling_row = total[1:2, :] / width_all * inverse_row * inverse_row
    first_label = row_of(states, 0, base + FIRST)
    second_label = row_of(states, 1, base + FIRST)
    inverse = [as_columns(inverse_row[:, c * rows : (c + 1) * rows], rows) for c in range(2)]
    coupling = [as_columns(coupling_row[:, c * rows : (c + 1) * rows], rows) for c in range(2)]
    for h in range(heads):
        at = slice(h * width, (h + 1) * width)
        of_cores, of_both = [], []
        for c in range(2):
            _, _, scaled = token_rows(asked.at[c], made.at[c], h, heads, rows)
            value = inverse[c] * (scaled - attended[c, h] * coupling[c])
            of_both.append(value)
            of_cores.append(dot3((start_high[c, h], start_low[c, h]), split(value), NN))
        grad[h] = pick(second, of_both[1], of_both[0])
        back[at, :] = of_cores[1]
        passed = link(first_label, second_label, row_of(states, 0, base + h))
        out[at, :] = of_cores[0] + passed * of_cores[1]
    chip_meta(states, out, base, heads)


def main_grad_body(
    queries, keys, values, decay, docs, within, weighted, grad, states, arrived, sent,
    query_grad, key_local, value_local, tails, *halves,
):
    del sent
    rows, width = queries.shape[1:]
    base = arrived.shape[1] - EXTRA
    lower = lower_mask(rows)
    second = lax.axis_index("core") == 1
    near = pick(second, row_of(states, 0, base + LAST), row_of(arrived, 0, base + LAST))
    ahead = as_columns(docs[...].astype(F32), rows) == near
    for h in range(queries.shape[0]):
        of_grad = split(grad[h])
        of_keys = split(keys[h])
        of_values = split(values[h])
        of_both = split(within[h] * dot3(of_grad, of_values, NT))
        cumulative = running(lower, decay[h : h + 1, :])
        outer_state, inner_state = states_ahead(states, arrived, h, width)
        of_state = split(pick(second, inner_state, outer_state))
        reach = jnp.where(ahead, jnp.exp(cumulative), 0.0)
        query_grad[h] = dot3(of_both, of_keys, NN) + reach * dot3(of_grad, of_state, NT)
        key_local[h] = dot3(of_both, split(queries[h]), TN)
        value_local[h] = dot3(split(weighted[h]), of_grad, TN)
        for half, part in zip(halves, (*of_keys, *of_values)):
            half[h] = part
        tail = jnp.exp(cumulative[rows - 1 :, :] - cumulative)
        tails[h] = jnp.broadcast_to(tail, tails.shape[1:])


def last_grad_body(
    keys_high, keys_low, values_high, values_low, tails, docs, key_local, value_local,
    meta, back, arrived, key_grad_hbm, value_grad_hbm, key_grad, value_grad, sent,
):
    heads, rows, width = tails.shape
    base = heads * width
    first = lax.axis_index("core") == 0
    near = row_of(arrived, 0, base + FIRST)
    chained = near == row_of(arrived, 1, base + FIRST)
    inner = row_of(meta, 1, base + FIRST)
    linked = inner == near
    ahead = as_columns(docs[...].astype(F32), rows) == jnp.where(first, inner, near)
    copies = []
    for h in range(heads):
        at = slice(h * width, (h + 1) * width)
        weight = jnp.where(chained, jnp.exp(row_of(arrived, 0, base + h)), 0.0)
        state = arrived[0, at, :] + weight * arrived[1, at, :]
        passed = jnp.where(linked, jnp.exp(row_of(meta, 1, base + h)), 0.0)
        of_state = split(jnp.where(first, back[at, :] + passed * state, state))
        to_next = jnp.where(ahead, tails[h], 0.0)
        key_grad[h] = key_local[h] + to_next * dot3((values_high[h], values_low[h]), of_state, NT)
        value_grad[h] = value_local[h] + to_next * dot3((keys_high[h], keys_low[h]), of_state, NN)
        if h < heads - 2:
            continue
        for i, (a, b) in enumerate(((key_grad, key_grad_hbm), (value_grad, value_grad_hbm))):
            done = slice(0 if h < heads - 1 else h, h + 1)
            copies.append(pltpu.make_async_copy(a.at[done], b.at[done], sent.at[2 * (h - heads + 2) + i]))
            copies[-1].start()
    for copy in copies:
        copy.wait()


def per_device(queries, keys, values, out_grad, norm_gain, log_decay, doc_ids):
    heads, rows, width = queries.shape
    seq = lax.axis_size("chip") * 2
    group = lax.axis_size("head")
    docs = doc_ids.reshape(1, rows)
    shape = lambda *dims: jax.ShapeDtypeStruct(dims, F32)
    block = shape(heads, rows, width)
    payload = shape(heads * width + EXTRA, width)
    product = 6 * heads * rows * width * width

    given = [keys, values, norm_gain, log_decay, docs]
    own, keys, values, norm_gain, log_decay, docs = kernel_call(
        state_body,
        (payload, *(jax.ShapeDtypeStruct(a.shape, a.dtype) for a in given)),
        product,
        "h" * len(given),
        scratch=(pltpu.SemaphoreType.DMA((len(given),)),),
    )(*(pltpu.with_memory_space_constraint(a, pltpu.HBM) for a in given))
    states = lax.all_gather(own, "core")
    chip_state = kernel_call(functools.partial(forward_join_body, heads), payload, product // 64)(states)
    ahead = [(i, i + 2 + 2 * (i % 2)) for i in range(seq)]
    moved = lax.ppermute(chip_state, ("chip", "core"), [(a, b) for a, b in ahead if b < seq])
    more = heads // 2 * rows
    asked, made, within, weighted = kernel_call(
        local_body,
        (
            shape(heads * rows + more + EXTRA, width),
            shape(2 * heads * rows - more, width),
            block,
            block,
        ),
        2 * product,
    )(queries, keys, values, out_grad, norm_gain, log_decay, docs, chip_state)
    asked = lax.all_gather(asked, "core")
    made, asked = lax.optimization_barrier((made, asked))
    made = lax.all_gather(made, "core")
    twice = shape(2, heads, rows, width)
    halves_twice = jax.ShapeDtypeStruct(twice.shape, BF16)
    high, low, start_high, start_low, passes = kernel_call(
        prepare_body, (halves_twice,) * 4 + (twice,), product // 4
    )(asked, states)
    moved, made, passes = lax.optimization_barrier((moved, made, passes))
    arrived = lax.all_gather(moved, "core")
    attended, sums = kernel_call(
        attended_body, (twice, shape(group, 2, 2 * rows)), 2 * product
    )(asked, made, states, high, low, passes, arrived)
    sums = lax.all_to_all(sums, "head", 0, 0, tiled=True)
    grad, chip_back, back = kernel_call(
        functools.partial(grad_state_body, heads * width * group),
        (block, payload, shape(heads * width, width)),
        2 * product,
    )(sums, attended, asked, made, states, start_high, start_low)
    behind = [(i, i - 2 - 2 * (i % 2)) for i in range(seq)]
    moved_back = lax.ppermute(chip_back, ("chip", "core"), [(a, b) for a, b in behind if b >= 0])
    half = jax.ShapeDtypeStruct((heads, rows, width), BF16)
    query_grad, key_local, value_local, tails, *halves = kernel_call(
        main_grad_body, (block,) * 4 + (half,) * 4, 5 * product
    )(
        queries, keys, values, log_decay, docs, within, weighted, grad, states, arrived, chip_back
    )
    arrived_back = lax.all_gather(moved_back, "core")
    held = pltpu.VMEM((heads, rows, width), F32)
    key_grad, value_grad = kernel_call(
        last_grad_body,
        (block,) * 2,
        2 * product,
        "",
        "hh",
        (held, held, pltpu.SemaphoreType.DMA((heads,))),
    )(*halves, tails, docs, key_local, value_local, states, back, arrived_back)
    return query_grad, key_grad, value_grad


def solution(mesh):
    seq, head = mesh.devices.shape
    fine = Mesh(mesh.devices.reshape(seq // 2, 2, head), ("chip", "core", "head"))
    tokens = ("chip", "core")
    block = P("head", tokens, None)
    return jax.shard_map(
        per_device,
        mesh=fine,
        in_specs=(block, block, block, block, P("head", None), P("head", tokens), P(tokens)),
        out_specs=(block, block, block),
        check_vma=False,
    )
```
